32 devices in a mesh: dp: 2 (over y), row: 4 (over z), col: 4 (over x, core).
Axes of the slice: x: 2, y: 2, z: 4, core: 2. Of those that a mesh axis runs over, the one named last changes fastest.
Arguments:
- tokens: bfloat16 [2, 16384, 1472], P(None, ('dp', 'row', 'col')), may hold values from -6 to 6
- out_grad: bfloat16 [2, 16384, 1472], P(None, ('dp', 'row', 'col')), may hold values from -6 to 6
- lengths: int32 [2, 32, 2], P(None, ('dp', 'row', 'col')), may hold values from 1 to 384, 512 in all within a row
- offset_bucket: int32 [1023], replicated, may hold values from 0 to 31
- qkv_weight: bfloat16 [1472, 1152], P('dp'), may hold values from -0.078125 to 0.078125
- out_weight: bfloat16 [384, 1472], P(None, 'dp'), may hold values from -1.25 to 1.25
- bias_table: bfloat16 [32, 6], P('dp'), may hold values from -4 to 4
- norm_gains: bfloat16 [2, 1472], P(None, 'dp'), may hold values from 0.5 to 1.5
- inner_weight: bfloat16 [2, 1472, 3584], P(None, ('dp', 'row'), 'col'), may hold values from -0.15625 to 0.15625
- outer_weight: bfloat16 [3584, 1472], P('col', ('dp', 'row')), may hold values from -0.09375 to 0.09375
Outputs:
- layer_out: bfloat16 [2, 16384, 1472], P(None, ('dp', 'row', 'col'))
- tokens_grad: bfloat16 [2, 16384, 1472], P(None, ('dp', 'row', 'col'))
- qkv_grad: float32 [1472, 1152], P('dp')
- out_weight_grad: float32 [384, 1472], P(None, 'dp')
- table_grad: float32 [32, 6], P('dp')
- gains_grad: float32 [2, 1472], P(None, 'dp')
- inner_grad: float32 [2, 1472, 3584], P(None, ('dp', 'row'), 'col')
- outer_grad: float32 [3584, 1472], P('col', ('dp', 'row'))
The draws below stay inside these ranges and needn't reach their ends.
Inputs may be any that keep to these rules, and one draw needn't show every extreme that they name: Each row holds the lengths of 2 documents that fill one device's 512 tokens of one micro-batch exactly; in each row the longest has at most 384 tokens.
All inputs are finite; a program needn't handle non-finite values.
Results may differ from the reference program's by a relative error of at most 0.029.
Values may be sent and summed in bfloat16 or wider, within the bound.
A program may use at most 152 MiB of HBM per device.

```python
import math
import jax
import jax.numpy as jnp
import numpy as np
from jax import lax

D = 1472
FF = 3584
HEADS = 6
HEAD_DIM = 64
BUCKETS = 32
CAP = 512
SLOTS = 2
MICRO = 2
TOK_MB = 16384
DEVICES = 32


def with_ends(values, rng, least, top_value):
    longest = values.shape.index(max(values.shape))
    spots = []
    for shift in (0, 1):
        where = [jax.random.randint(jax.random.fold_in(rng, axis), (), 0, length) for axis, length in enumerate(values.shape)]
        where[longest] = (where[longest] + shift) % values.shape[longest]
        spots.append(tuple(where))
    return values.at[spots[0]].set(least).at[spots[1]].set(top_value)


def steps_of(stream_key, shape, split, least, largest):
    def one(position, shards_of):
        steps = jax.random.uniform(jax.random.fold_in(jax.random.fold_in(stream_key, 6), position), (shards_of,), jnp.float32, least / len(split), largest / len(split))
        return jnp.repeat(jnp.exp(steps), shape[position] // shards_of).reshape((-1,) + (1,) * (len(shape) - position - 1))

    loudness = one(*split[0])
    for cut in split[1:]:
        loudness = loudness * one(*cut)
    return loudness


def profile(number_of, total, most, slope):
    weights = [(1 << 20) // math.isqrt(grade ** slope) + 1 for grade in range(2, number_of + 1)]
    spare, given = total - most - (number_of - 1), [1] * (number_of - 1)
    while spare > 0:
        movable = [i for i in range(number_of - 1) if given[i] < most]
        whole, remaining = sum([weights[i] for i in movable]), spare
        for i in movable:
            more = min(most - given[i], max(1, remaining * weights[i] // whole), spare)
            given[i] = given[i] + more
            spare = spare - more
    return np.array([most] + given)


def uneven_parts(rng, amount, total, most, skew):
    if amount == 2:
        one = jax.random.randint(rng, (), max(1, total - most), min(most, total - 1) + 1)
        return jnp.stack([one, total - one])
    sizes = jnp.asarray(profile(amount, total, most, skew), jnp.int32)
    couples = (amount - 1) // 2
    source_of, taker = sizes[1:1 + 2 * couples:2], sizes[2:2 + 2 * couples:2]
    margin = jnp.minimum(source_of - 1, most - taker)
    moved = jax.random.randint(jax.random.fold_in(rng, 1), (couples,), 0, 1 << 20) % (margin + 1)
    sizes = sizes.at[1:1 + 2 * couples:2].set(source_of - moved).at[2:2 + 2 * couples:2].set(taker + moved)
    return sizes[jax.random.permutation(jax.random.fold_in(rng, 2), amount)]


def centred(stream_key, dims, scale, bound, pieces=(), held_as=jnp.bfloat16):
    loudness = steps_of(stream_key, dims, pieces, -0.22, 0.18) if pieces else 1.0
    values = jax.random.normal(stream_key, dims, jnp.float32) * scale * loudness
    return jnp.minimum(jnp.maximum(values, -bound), bound).astype(held_as)


def setup_inputs(seed: int = 0) -> dict:
    key_list = jax.random.split(jax.random.key(seed), 11)
    return {
        "tokens": centred(key_list[0], (MICRO, TOK_MB, D), 1.0, 6.0, ((1, 32),)),
        "out_grad": centred(key_list[1], (MICRO, TOK_MB, D), 1.0, 6.0, ((1, 32),)),
        "lengths": jax.vmap(lambda own: uneven_parts(own, SLOTS, CAP, CAP * 3 // 4, 1))(jax.random.split(key_list[2], MICRO * DEVICES)).reshape((MICRO, DEVICES, SLOTS)).astype(jnp.int32),
        "offset_bucket": with_ends(jax.random.randint(key_list[3], (2 * CAP - 1,), 0, BUCKETS), jax.random.fold_in(key_list[3], 1), 0, BUCKETS - 1).astype(jnp.int32),
        "qkv_weight": centred(key_list[4], (D, 3 * HEADS * HEAD_DIM), (4 * D) ** -0.5, 0.078125, ((0, 2),)),
        "out_weight": centred(key_list[5], (HEADS * HEAD_DIM, D), (HEADS * HEAD_DIM // 16) ** -0.5, 1.25, ((1, 2),)),
        "bias_table": centred(key_list[6], (BUCKETS, HEADS), 1.0, 4.0, ((0, 2),)),
        "norm_gains": jnp.clip(1.0 + 0.1 * jax.random.normal(key_list[7], (2, D), jnp.float32), 0.5, 1.5).astype(jnp.bfloat16),
        "inner_weight": centred(key_list[8], (2, D, FF), D ** -0.5, 0.15625, ((1, 8), (2, 4))),
        "outer_weight": centred(key_list[9], (FF, D), FF ** -0.5, 0.09375, ((0, 4), (1, 8))),
    }


epsilon = 1e-06
masked_score = -1000000000.0
highest = lax.Precision.HIGHEST

@jax.custom_vjp
def low(v):
    return lax.optimization_barrier(v.astype(jnp.bfloat16)).astype(jnp.float32)

@jax.custom_vjp
def low_back(v):
    return v

def low_keep(v):
    return (low(v), None)

def low_pass(kept, grad):
    return (grad,)

def back_keep(v):
    return (v, None)

def back_low(kept, grad):
    return (low(grad),)
low.defvjp(low_keep, low_pass)
low_back.defvjp(back_keep, back_low)

def rms_normed(values, gain):
    scale = lax.rsqrt(lax.optimization_barrier(jnp.mean(values * values, axis=1, keepdims=True)) + epsilon)
    return values * scale * gain

def block_layer(weights, block_tokens, doc_lengths, offset_bucket):
    qkv_w, out_w, table, gains, inner_w, outer_w = weights
    row_count = block_tokens.shape[0]
    inner_width = HEADS * HEAD_DIM
    places = jnp.arange(row_count, dtype=jnp.int32)
    doc_ends = jnp.cumsum(doc_lengths).astype(jnp.int32)
    labels = lax.optimization_barrier(jnp.sum((places[:, None] >= doc_ends[None, :]).astype(jnp.int32), axis=1))
    same_doc = labels[:, None] == labels[None, :]
    normed_one = low(rms_normed(block_tokens, gains[0]))
    qkv_rows = low(low_back(jnp.dot(normed_one, qkv_w, precision=highest)))
    queries = qkv_rows[:, :inner_width].reshape(row_count, HEADS, HEAD_DIM)
    key_rows = qkv_rows[:, inner_width:2 * inner_width].reshape(row_count, HEADS, HEAD_DIM)
    value_rows = qkv_rows[:, 2 * inner_width:].reshape(row_count, HEADS, HEAD_DIM)
    offset_bias = jnp.take(table, offset_bucket, axis=0)
    offsets = (places[None, :] - places[:, None] + row_count - 1).astype(jnp.int32)
    score_bias = jnp.transpose(jnp.take(offset_bias, offsets, axis=0), (2, 0, 1))
    scores = low_back(jnp.einsum('ihd,jhd->hij', queries, key_rows, precision=highest) + score_bias)
    scores = jnp.where(same_doc[None], scores, masked_score)
    attn_low = low(jax.nn.softmax(scores, axis=-1))
    attended = jnp.einsum('hij,jhd->ihd', attn_low, value_rows, precision=highest).reshape(row_count, inner_width)
    attended = low(low_back(attended))
    residual = block_tokens + low_back(jnp.dot(attended, out_w, precision=highest))
    normed_two = low(rms_normed(residual, gains[1]))
    gate_pre = low_back(jnp.dot(normed_two, inner_w[0], precision=highest))
    up_pre = low_back(jnp.dot(normed_two, inner_w[1], precision=highest))
    hidden = low(jax.nn.gelu(gate_pre, approximate=True) * up_pre)
    branch = low_back(jnp.dot(hidden, outer_w, precision=highest))
    return residual + branch

def forward(all_tokens, qkv_w, out_w, table, gains, inner_w, outer_w, all_lengths, offset_bucket):
    weights = (qkv_w, out_w, table, gains, inner_w, outer_w)

    def one_block(pair):
        return block_layer(weights, pair[0], pair[1], offset_bucket)
    return lax.map(jax.checkpoint(one_block), (all_tokens, all_lengths))

def reference(tokens, out_grad, lengths, offset_bucket, qkv_weight, out_weight, bias_table, norm_gains, inner_weight, outer_weight):
    blocks = tokens.astype(jnp.float32).reshape(-1, CAP, D)
    all_lengths = lengths.reshape(-1, SLOTS)
    primal = (blocks, qkv_weight.astype(jnp.float32), out_weight.astype(jnp.float32), bias_table.astype(jnp.float32), norm_gains.astype(jnp.float32), inner_weight.astype(jnp.float32), outer_weight.astype(jnp.float32))

    def run_layer(block_tokens, qkv_w, out_w, table, gains, inner_w, outer_w):
        return forward(block_tokens, qkv_w, out_w, table, gains, inner_w, outer_w, all_lengths, offset_bucket)
    result, pull_back = jax.vjp(run_layer, *primal)
    grads = pull_back(out_grad.astype(jnp.float32).reshape(-1, CAP, D))
    layer_out = result.reshape(tokens.shape).astype(jnp.bfloat16)
    tokens_grad = grads[0].reshape(tokens.shape).astype(jnp.bfloat16)
    return (layer_out, tokens_grad, grads[1], grads[2], grads[3], grads[4], grads[5], grads[6])
```

```python
import functools

import jax
import jax.numpy as jnp
from jax import lax
from jax.experimental import pallas as pl
from jax.experimental.pallas import tpu as pltpu
from jax.sharding import PartitionSpec as P

epsilon = 1e-06
masked_score = -1000000000.0
highest = lax.Precision.HIGHEST
gelu_scale = 0.7978845608028654
gelu_cubic = 0.044715
MESH = pl.DeviceIdType.MESH
f32 = jnp.float32
bf16 = jnp.bfloat16
tile = 128
vmem_bytes = 63 * 1024 * 1024


def dot_nn(a, b):
    return lax.dot_general(a, b, (((1,), (0,)), ((), ())), preferred_element_type=f32)


def dot_nt(a, b):
    return lax.dot_general(a, b, (((1,), (1,)), ((), ())), preferred_element_type=f32)


def dot_tn(a, b):
    return lax.dot_general(a, b, (((0,), (0,)), ((), ())), preferred_element_type=f32)


def bucket_onehot(bucket_ref, bucket_count):
    span = bucket_ref.shape[1]
    ids = lax.broadcasted_iota(jnp.int32, (bucket_count, span), 0)
    return ids == jnp.broadcast_to(bucket_ref[0:1, :], (bucket_count, span))


def fill_bias_tiles(tables, bucket_ref, tiles_ref):
    head_count, diag_count = tiles_ref.shape[:2]
    bucket_count = sum(table.shape[1] for table in tables)
    onehot = bucket_onehot(bucket_ref, bucket_count).astype(f32)
    rev = None
    start = 0
    for table in tables:
        stop = start + table.shape[1]
        part = dot_nn(table, onehot[start:stop].astype(bf16))
        rev = part if rev is None else rev + part
        start = stop
    for h in range(head_count):
        for d in range(diag_count):
            row = rev[h : h + 1, tile * d : tile * d + 2 * tile]
            wide = jnp.broadcast_to(row, (tile, 2 * tile))
            turned = pltpu.roll(wide, tile + 1, 1, stride=1, stride_axis=0)[:, :tile]
            tiles_ref[h, d] = turned.astype(tiles_ref.dtype)


def bias_block(tiles_ref, h, key_block, blocks):
    return jnp.concatenate(
        [tiles_ref[h, q - key_block + blocks - 1] for q in range(blocks)], axis=1
    )


def doc_labels(lens_ref, axis, rows):
    shape = (rows, 1) if axis == 0 else (1, rows)
    place = lax.broadcasted_iota(jnp.int32, shape, axis)
    label = jnp.zeros(shape, jnp.int32)
    end = jnp.int32(0)
    for slot in range(lens_ref.shape[2]):
        end = end + lens_ref[0, 0, slot]
        label = label + (place >= end).astype(jnp.int32)
    return label


def masked_scores(key_rows, query_cols, tiles_ref, h, same_doc, blocks):
    raw = dot_nn(key_rows, query_cols)
    bias = jnp.concatenate([bias_block(tiles_ref, h, kb, blocks) for kb in range(blocks)], axis=0)
    return jnp.where(same_doc, raw + bias.astype(f32), masked_score)


def pad_cotangent(og_ref, og_pad_ref, og_pad_t_ref, shard_rows, pad_rows):
    model, rows = og_ref.shape[1:]
    for k in range(model // shard_rows):
        part = slice(k * shard_rows, (k + 1) * shard_rows)
        og_pad_t_ref[k * pad_rows : k * pad_rows + shard_rows, :] = (
            og_ref[0, part, :].astype(f32).astype(bf16)
        )
        rest = slice(k * pad_rows + shard_rows, (k + 1) * pad_rows)
        if pad_rows > shard_rows:
            og_pad_t_ref[rest, :] = jnp.zeros((pad_rows - shard_rows, rows), bf16)
    og_pad_ref[...] = og_pad_t_ref[...].T


def attend(
    lens_ref,
    tok_ref,
    qkv_w_ref,
    out_w_ref,
    gains_ref,
    normed_ref,
    normed_t_ref,
    qkv_ref,
    attended_ref,
    log_ref,
    residual_ref,
    tiles_ref,
    scaled_ref,
    shard_rows,
    pad_rows,
    between,
):
    model, rows = tok_ref.shape[1:]
    inner = attended_ref.shape[1]
    head_count = tiles_ref.shape[0]
    head_dim = inner // head_count
    blocks = rows // tile
    parts = model // shard_rows
    slabs, slab_rows = qkv_w_ref.shape[:2]

    square = jnp.zeros((1, rows), f32)
    for k in range(parts):
        x = tok_ref[0, k * shard_rows : (k + 1) * shard_rows, :].astype(f32)
        square = square + jnp.sum(x * x, axis=0, keepdims=True)
    scale = lax.rsqrt(square / model + epsilon)
    for k in range(parts):
        part = slice(k * shard_rows, (k + 1) * shard_rows)
        x = tok_ref[0, part, :].astype(f32)
        scaled_ref[part, :] = x * scale * gains_ref[part, 0:1]
    total = None
    for slab in range(slabs):
        normed = scaled_ref[slab * slab_rows : (slab + 1) * slab_rows, :].astype(bf16)
        product = dot_tn(qkv_w_ref[slab], normed)
        total = product if total is None else total + product
    qkv_ref[0] = total.astype(bf16)

    same_doc = doc_labels(lens_ref, 0, rows) == doc_labels(lens_ref, 1, rows)

    def head(h, carry):
        base = pl.multiple_of(h * head_dim, head_dim)
        query_cols = qkv_ref[0, pl.ds(base, head_dim), :]
        key_cols = qkv_ref[0, pl.ds(inner + base, head_dim), :]
        value_cols = qkv_ref[0, pl.ds(2 * inner + base, head_dim), :]
        scores = masked_scores(key_cols.T, query_cols, tiles_ref, h, same_doc, blocks)
        peak = jnp.max(scores, axis=0, keepdims=True)
        weight = jnp.exp(scores - peak)
        total = jnp.sum(weight, axis=0, keepdims=True)
        low = (weight * (1.0 / total)).astype(bf16)
        attended_ref[0, pl.ds(base, head_dim), :] = dot_nn(value_cols, low).astype(bf16)
        log_ref[0, h] = jnp.broadcast_to(peak + jnp.log(total), (8, rows))
        return carry

    lax.fori_loop(0, head_count, head, 0)
    between()

    for slab in range(slabs):
        scaled_ref[slab * slab_rows : (slab + 1) * slab_rows, :] = dot_nn(
            out_w_ref[slab], attended_ref[0]
        )
    square = jnp.zeros((1, rows), f32)
    for k in range(parts):
        part = slice(k * shard_rows, (k + 1) * shard_rows)
        x = scaled_ref[part, :] + tok_ref[0, part, :].astype(f32)
        residual_ref[k * pad_rows : k * pad_rows + shard_rows, :] = x
        square = square + jnp.sum(x * x, axis=0, keepdims=True)
    scale = lax.rsqrt(square / model + epsilon)
    for k in range(parts):
        part = slice(k * shard_rows, (k + 1) * shard_rows)
        dest = slice(k * pad_rows, k * pad_rows + shard_rows)
        rest = slice(k * pad_rows + shard_rows, (k + 1) * pad_rows)
        x = residual_ref[dest, :]
        normed_t_ref[dest, :] = (x * scale * gains_ref[part, 1:2]).astype(bf16)
        if pad_rows > shard_rows:
            normed_t_ref[rest, :] = jnp.zeros((pad_rows - shard_rows, rows), bf16)
            residual_ref[rest, :] = jnp.zeros((pad_rows - shard_rows, rows), f32)
    normed_ref[...] = normed_t_ref[...].T


def attention_forward_kernel(
    lens_ref,
    tok_ref,
    og_ref,
    qkv_w_ref,
    out_w_ref,
    gains_ref,
    table_ref,
    bucket_ref,
    normed_ref,
    normed_t_ref,
    og_pad_ref,
    og_pad_t_ref,
    qkv_ref,
    attended_ref,
    log_ref,
    residual_ref,
    tiles_ref,
    scaled_ref,
    *,
    shard_rows,
    pad_rows,
):
    @pl.when(pl.program_id(0) == 0)
    def _():
        fill_bias_tiles([table_ref[...]], bucket_ref, tiles_ref)

    pad_cotangent(og_ref, og_pad_ref, og_pad_t_ref, shard_rows, pad_rows)
    attend(
        lens_ref, tok_ref, qkv_w_ref, out_w_ref, gains_ref, normed_ref, normed_t_ref, qkv_ref,
        attended_ref, log_ref, residual_ref, tiles_ref, scaled_ref, shard_rows, pad_rows,
        lambda: None,
    )


def forward_outputs(micro, heads, inner, model, rows, wide):
    once = lambda shape: pl.BlockSpec((1,) + shape, lambda m: (m,) + (0,) * len(shape))
    tokens = micro * rows
    across = pl.BlockSpec((rows, wide), lambda m: (m, 0))
    along = pl.BlockSpec((wide, rows), lambda m: (0, m))
    specs = [
        across, along, across, along, once((3 * inner, rows)), once((inner, rows)),
        once((heads, 8, rows)), along,
    ]
    shapes = [
        jax.ShapeDtypeStruct((tokens, wide), bf16),
        jax.ShapeDtypeStruct((wide, tokens), bf16),
        jax.ShapeDtypeStruct((tokens, wide), bf16),
        jax.ShapeDtypeStruct((wide, tokens), bf16),
        jax.ShapeDtypeStruct((micro, 3 * inner, rows), bf16),
        jax.ShapeDtypeStruct((micro, inner, rows), bf16),
        jax.ShapeDtypeStruct((micro, heads, 8, rows), f32),
        jax.ShapeDtypeStruct((wide, tokens), f32),
    ]
    return specs, shapes


def attention_forward(
    lens, tok, og, qkv_w, out_w, gains, table, bucket, heads, shard_rows, pad_rows
):
    micro, model, rows = tok.shape
    inner = out_w.shape[2]
    wide = model // shard_rows * pad_rows
    whole = pl.BlockSpec(memory_space=pltpu.VMEM)
    once = lambda shape: pl.BlockSpec((1,) + shape, lambda m: (m,) + (0,) * len(shape))
    out_specs, out_shape = forward_outputs(micro, heads, inner, model, rows, wide)
    return pl.pallas_call(
        functools.partial(attention_forward_kernel, shard_rows=shard_rows, pad_rows=pad_rows),
        grid=(micro,),
        in_specs=[
            pl.BlockSpec((1, 1, lens.shape[2]), lambda m: (m, 0, 0), memory_space=pltpu.SMEM),
            once((model, rows)),
            once((model, rows)),
            whole,
            whole,
            whole,
            whole,
            whole,
        ],
        out_specs=out_specs,
        out_shape=out_shape,
        scratch_shapes=[
            pltpu.VMEM((heads, 2 * (rows // tile) - 1, tile, tile), bf16),
            pltpu.VMEM((model, rows), f32),
        ],
        compiler_params=pltpu.CompilerParams(vmem_limit_bytes=vmem_bytes),
        name="attention_forward",
    )(lens, tok, og, qkv_w, out_w, gains, table, bucket)


class Hidden:
    block = 256
    span = 512

    def __init__(
        self, matrices, normed, normed_t, og, og_t, branch, back, hidden, gate, up, grad_of
    ):
        self.matrices = matrices
        self.normed, self.normed_t, self.og, self.og_t = normed, normed_t, og, og_t
        self.branch, self.back = branch, back
        self.hidden, self.gate, self.up = hidden, gate, up
        self.grad_of = grad_of

    def matrix(self, which, rows=slice(None)):
        return jnp.concatenate([part[rows, :] for part in self.matrices[which]], axis=1)

    def project(self, start, stop):
        def step(b, carry):
            rows = pl.ds(pl.multiple_of(b * self.block, self.block), self.block)
            gate = dot_nn(self.normed[rows, :], self.matrix(0))
            up = dot_nn(self.normed[rows, :], self.matrix(1))
            grad = dot_nn(self.og[rows, :], self.matrix(2))
            cube = gelu_cubic * gate * gate
            t = jnp.tanh(gelu_scale * gate * (1.0 + cube))
            half = 0.5 * (1.0 + t)
            act = gate * half
            slope = half + (0.5 * gelu_scale) * gate * (1.0 - t * t) * (1.0 + 3.0 * cube)
            self.hidden[rows, :] = (act * up).astype(bf16)
            self.gate[rows, :] = (grad * up * slope).astype(bf16)
            self.up[rows, :] = (grad * act).astype(bf16)
            return carry

        lax.fori_loop(start, stop, step, 0)

    def weights(self, start, stop):
        tokens = self.normed.shape[0]
        span = self.span

        def step(b, carry):
            rows = pl.ds(pl.multiple_of(b * span, span), span)
            for which, (left, right) in enumerate(
                (
                    (self.normed_t, self.gate),
                    (self.normed_t, self.up),
                    (self.og_t, self.hidden),
                )
            ):
                grad = dot_nn(left[rows, :], right[...]).astype(bf16)
                for j in range(len(self.matrices[which])):
                    self.grad_of(which, j)[rows, :] = grad[:, j * tile : (j + 1) * tile]
            for which, parts, into in (
                (2, (self.hidden,), self.branch),
                (0, (self.gate, self.up), self.back),
            ):
                for half in range(tokens // span):
                    cols = slice(half * span, (half + 1) * span)
                    total = into[rows, cols]
                    for offset, part in enumerate(parts):
                        total = total + dot_nt(self.matrix(which + offset, rows), part[cols, :])
                    into[rows, cols] = total
            return carry

        lax.fori_loop(start, stop, step, 0)


def feed_forward_kernel(
    normed_hbm,
    normed_t_hbm,
    og_hbm,
    og_t_hbm,
    residual_hbm,
    weight_ref,
    layer_ref,
    back_hbm,
    grad_ref,
    normed_ref,
    normed_t_ref,
    og_ref,
    og_t_ref,
    branch_ref,
    back_ref,
    hidden_ref,
    gate_ref,
    up_ref,
    sems,
    *,
    shard_rows,
    pad_rows,
):
    step = pl.program_id(0)
    col_count = weight_ref.shape[1]
    tokens = normed_ref.shape[0]
    wide = normed_ref.shape[1]
    copies = [
        pltpu.make_async_copy(normed_hbm, normed_ref, sems.at[0]),
        pltpu.make_async_copy(og_hbm, og_ref, sems.at[1]),
        pltpu.make_async_copy(normed_t_hbm, normed_t_ref, sems.at[2]),
        pltpu.make_async_copy(og_t_hbm, og_t_ref, sems.at[3]),
    ]

    @pl.when(step == 0)
    def _():
        fill = pltpu.make_async_copy(residual_hbm, branch_ref, sems.at[5])
        fill.start()
        for copy in copies:
            copy.start()
        for copy in copies:
            copy.wait()
        back_ref[...] = jnp.zeros(back_ref.shape, f32)
        fill.wait()

    matrices = [[weight_ref.at[0, j, which] for j in range(col_count)] for which in range(3)]
    unit = Hidden(
        matrices, normed_ref, normed_t_ref, og_ref, og_t_ref, branch_ref, back_ref, hidden_ref,
        gate_ref, up_ref, lambda which, j: grad_ref.at[0, j, which],
    )
    unit.project(0, tokens // unit.block)
    unit.weights(0, wide // unit.span)

    @pl.when(step == pl.num_programs(0) - 1)
    def _():
        out = pltpu.make_async_copy(back_ref, back_hbm, sems.at[4])
        out.start()
        micro, model, rows = layer_ref.shape
        for m in range(micro):
            for k in range(model // shard_rows):
                source = slice(k * pad_rows, k * pad_rows + shard_rows)
                part = slice(k * shard_rows, (k + 1) * shard_rows)
                layer_ref[m, part, :] = branch_ref[source, m * rows : (m + 1) * rows].astype(bf16)
        out.wait()


def feed_forward(
    normed, normed_t, og, og_t, residual, weights, micro, model, shard_rows, pad_rows
):
    tokens, wide = normed.shape
    rows = tokens // micro
    steps, col_count = weights.shape[:2]
    width = col_count * tile
    anywhere = pl.BlockSpec(memory_space=pl.ANY)
    per_step = lambda: pl.BlockSpec((1,) + weights.shape[1:], lambda t: (t, 0, 0, 0, 0))
    return pl.pallas_call(
        functools.partial(feed_forward_kernel, shard_rows=shard_rows, pad_rows=pad_rows),
        grid=(steps,),
        in_specs=[anywhere] * 5 + [per_step()],
        out_specs=[
            pl.BlockSpec((micro, model, rows), lambda t: (0, 0, 0)),
            anywhere,
            per_step(),
        ],
        out_shape=[
            jax.ShapeDtypeStruct((micro, model, rows), bf16),
            jax.ShapeDtypeStruct((wide, tokens), f32),
            jax.ShapeDtypeStruct(weights.shape, bf16),
        ],
        scratch_shapes=[
            pltpu.VMEM((tokens, wide), bf16),
            pltpu.VMEM((wide, tokens), bf16),
            pltpu.VMEM((tokens, wide), bf16),
            pltpu.VMEM((wide, tokens), bf16),
            pltpu.VMEM((wide, tokens), f32),
            pltpu.VMEM((wide, tokens), f32),
            pltpu.VMEM((tokens, width), bf16),
            pltpu.VMEM((tokens, width), bf16),
            pltpu.VMEM((tokens, width), bf16),
            pltpu.SemaphoreType.DMA((6,)),
        ],
        compiler_params=pltpu.CompilerParams(vmem_limit_bytes=vmem_bytes),
        name="feed_forward",
    )(normed, normed_t, og, og_t, residual, weights)


def lane_fold(values):
    total = values[:, :tile]
    for q in range(1, values.shape[1] // tile):
        total = total + values[:, q * tile : (q + 1) * tile]
    return total


def padded_spans(start, stop, shard_rows, pad_rows):
    spans = []
    while start < stop:
        group, offset = divmod(start, shard_rows)
        size = min(stop - start, shard_rows - offset)
        spans.append((group * pad_rows + offset, size))
        start += size
    return spans


class Padded:
    def __init__(self, ref, shard_rows, pad_rows):
        self.ref, self.shard_rows, self.pad_rows = ref, shard_rows, pad_rows

    def read(self, start, stop):
        spans = padded_spans(start, stop, self.shard_rows, self.pad_rows)
        return jnp.concatenate([self.ref[at : at + size, :] for at, size in spans], axis=0)

    def write(self, start, stop, value):
        done = 0
        for at, size in padded_spans(start, stop, self.shard_rows, self.pad_rows):
            self.ref[at : at + size, :] = value[done : done + size]
            done += size


def attend_back(
    lens_ref,
    tok_ref,
    og_ref,
    wide_ref,
    back_ref,
    qkv_ref,
    attended_ref,
    log_ref,
    qkv_w_ref,
    out_w_ref,
    gains_ref,
    tok_grad_ref,
    tiles_ref,
    diag_ref,
    low_ref,
    grad_qkv_ref,
    fold_ref,
    add_out,
    add_qkv,
    before_heads,
    after_heads,
):
    model, rows = tok_ref.shape[1:]
    inner = attended_ref.shape[1]
    head_count = tiles_ref.shape[0]
    head_dim = inner // head_count
    blocks = rows // tile
    diag_count = 2 * blocks - 1
    size = model // 4
    quarters = [(k * size, (k + 1) * size) for k in range(4)]

    square = jnp.zeros((1, rows), f32)
    cross = jnp.zeros((1, rows), f32)
    for start, stop in quarters:
        x = wide_ref.read(start, stop)
        y = back_ref.read(start, stop)
        square = square + jnp.sum(x * x, axis=0, keepdims=True)
        cross = cross + jnp.sum(x * (y * gains_ref[start:stop, 1:2]), axis=0, keepdims=True)
    scale = lax.rsqrt(square / model + epsilon)
    pull = scale * scale * scale * (cross / model)
    for start, stop in quarters:
        x = wide_ref.read(start, stop)
        y = back_ref.read(start, stop)
        grad = og_ref[0, start:stop, :].astype(f32)
        grad = grad + scale * (y * gains_ref[start:stop, 1:2]) - x * pull
        wide_ref.write(start, stop, grad)
        low_ref[start:stop, :] = grad.astype(bf16)
        fold_ref[1, start:stop, :] += lane_fold(x * scale * y)
    for k, (start, stop) in enumerate(quarters):
        add_out(k, dot_nt(low_ref[start:stop, :], attended_ref[0]))
    grad_attended = dot_tn(out_w_ref[...], low_ref[...]).astype(bf16)
    grad_qkv_ref[0:inner, :] = grad_attended
    before_heads()

    same_doc = doc_labels(lens_ref, 0, rows) == doc_labels(lens_ref, 1, rows)

    def head(h, carry):
        base = pl.multiple_of(h * head_dim, head_dim)
        query_cols = qkv_ref[0, pl.ds(base, head_dim), :]
        key_cols = qkv_ref[0, pl.ds(inner + base, head_dim), :]
        value_cols = qkv_ref[0, pl.ds(2 * inner + base, head_dim), :]
        grad_cols = grad_qkv_ref[pl.ds(base, head_dim), :]
        scores = masked_scores(key_cols.T, query_cols, tiles_ref, h, same_doc, blocks)
        probs = jnp.exp(scores - log_ref[0, h, 0:1, :])
        grad_probs = dot_nn(value_cols.T, grad_cols)
        delta = jnp.sum(probs * grad_probs, axis=0, keepdims=True)
        grad_scores = (probs * (grad_probs - delta)).astype(bf16)
        grad_qkv_ref[pl.ds(2 * inner + base, head_dim), :] = dot_nt(
            grad_cols, probs.astype(bf16)
        ).astype(bf16)
        grad_qkv_ref[pl.ds(base, head_dim), :] = dot_nn(key_cols, grad_scores).astype(bf16)
        grad_qkv_ref[pl.ds(inner + base, head_dim), :] = dot_nt(query_cols, grad_scores).astype(
            bf16
        )
        wide = grad_scores.astype(f32)
        for d in range(diag_count):
            total = None
            for key_block in range(blocks):
                query_block = d - (blocks - 1) + key_block
                if 0 <= query_block < blocks:
                    piece = wide[
                        key_block * tile : (key_block + 1) * tile,
                        query_block * tile : (query_block + 1) * tile,
                    ]
                    total = piece if total is None else total + piece
            diag_ref[h, d] += total
        return carry

    lax.fori_loop(0, head_count, head, 0)
    after_heads()

    square = jnp.zeros((1, rows), f32)
    for start, stop in quarters:
        x = tok_ref[0, start:stop, :].astype(f32)
        square = square + jnp.sum(x * x, axis=0, keepdims=True)
    scale = lax.rsqrt(square / model + epsilon)
    cross = jnp.zeros((1, rows), f32)
    for k, (start, stop) in enumerate(quarters):
        x = tok_ref[0, start:stop, :].astype(f32)
        normed = (x * scale * gains_ref[start:stop, 0:1]).astype(bf16)
        add_qkv(k, dot_nt(normed, grad_qkv_ref[...]))
        y = dot_nn(qkv_w_ref[start:stop, :], grad_qkv_ref[...])
        back_ref.write(start, stop, y)
        cross = cross + jnp.sum(x * (y * gains_ref[start:stop, 0:1]), axis=0, keepdims=True)
        fold_ref[0, start:stop, :] += lane_fold(x * scale * y)
    pull = scale * scale * scale * (cross / model)
    for start, stop in quarters:
        x = tok_ref[0, start:stop, :].astype(f32)
        y = back_ref.read(start, stop)
        grad = wide_ref.read(start, stop) + scale * (y * gains_ref[start:stop, 0:1]) - x * pull
        tok_grad_ref[0, start:stop, :] = grad.astype(bf16)


def dot_exact(a, b, dims):
    return lax.dot_general(
        a, b, ((dims[:1], dims[1:]), ((), ())), preferred_element_type=f32, precision=highest
    )


def bucket_sums(diag_ref, bucket_ref, bucket_count, head_rows):
    head_count, diag_count = diag_ref.shape[:2]
    down = lax.broadcasted_iota(jnp.int32, (tile, tile), 0)
    across = lax.broadcasted_iota(jnp.int32, (tile, tile), 1)
    flip = (down + across == tile - 1).astype(f32)
    onehot = bucket_onehot(bucket_ref, bucket_count).astype(f32)
    rest = jnp.zeros((tile, tile), f32)
    lines = []
    for h in range(head_count):
        carry = jnp.zeros((1, tile), f32)
        pieces = []
        for d in range(diag_count):
            turned = dot_exact(flip, diag_ref[h, d], (1, 0))
            spread = pltpu.roll(
                jnp.concatenate([turned, rest], axis=1), 0, 1, stride=1, stride_axis=0
            )
            sums = jnp.sum(spread, axis=0, keepdims=True)
            pieces.append(sums[:, :tile] + carry)
            carry = sums[:, tile:]
        pieces.append(carry)
        lines.append(jnp.concatenate(pieces, axis=1))
    filler = jnp.zeros((head_rows - head_count, onehot.shape[1]), f32)
    return dot_exact(jnp.concatenate(lines + [filler], axis=0), onehot, (1, 1))


def gain_rows_of(fold_ref, start, stop):
    down = lax.broadcasted_iota(jnp.int32, (16, 2 * tile), 0)
    across = lax.broadcasted_iota(jnp.int32, (16, 2 * tile), 1)
    pick = (across // tile == down).astype(f32)
    both = jnp.concatenate([fold_ref[0, start:stop, :], fold_ref[1, start:stop, :]], axis=1)
    return dot_exact(pick, both, (1, 1))


def attention_backward_kernel(
    lens_ref,
    tok_ref,
    og_ref,
    residual_hbm,
    back_hbm,
    qkv_ref,
    attended_ref,
    log_ref,
    qkv_w_ref,
    out_w_ref,
    gains_ref,
    table_ref,
    bucket_ref,
    tok_grad_ref,
    qkv_grad_ref,
    out_grad_ref,
    table_grad_ref,
    gains_grad_ref,
    wide_ref,
    back_ref,
    tiles_ref,
    diag_ref,
    low_ref,
    grad_qkv_ref,
    fold_ref,
    sems,
    *,
    shard_rows,
    pad_rows,
):
    micro_index = pl.program_id(0)
    model, rows = tok_ref.shape[1:]
    size = model // 4
    start_load(residual_hbm, back_hbm, wide_ref, back_ref, sems, micro_index)

    @pl.when(micro_index == 0)
    def _():
        fill_bias_tiles([table_ref[...]], bucket_ref, tiles_ref)
        diag_ref[...] = jnp.zeros(diag_ref.shape, f32)
        fold_ref[...] = jnp.zeros(fold_ref.shape, f32)
        qkv_grad_ref[...] = jnp.zeros(qkv_grad_ref.shape, f32)
        out_grad_ref[...] = jnp.zeros(out_grad_ref.shape, f32)

    wait_load(residual_hbm, back_hbm, wide_ref, back_ref, sems, micro_index)

    def add_out(k, value):
        out_grad_ref[k * size : (k + 1) * size, :] += value

    def add_qkv(k, value):
        qkv_grad_ref[k * size : (k + 1) * size, :] += value

    nothing = lambda: None
    attend_back(
        lens_ref, tok_ref, og_ref, Padded(wide_ref, shard_rows, pad_rows),
        Padded(back_ref, shard_rows, pad_rows), qkv_ref, attended_ref, log_ref, qkv_w_ref,
        out_w_ref, gains_ref, tok_grad_ref, tiles_ref, diag_ref, low_ref, grad_qkv_ref, fold_ref,
        add_out, add_qkv, nothing, nothing,
    )

    @pl.when(micro_index == pl.num_programs(0) - 1)
    def _():
        gains_grad_ref[...] = gain_rows_of(fold_ref, 0, model)
        head_rows, bucket_count = table_grad_ref.shape
        table_grad_ref[...] = bucket_sums(diag_ref, bucket_ref, bucket_count, head_rows)


def load_copies(residual_hbm, back_hbm, wide_ref, back_ref, sems, m):
    rows = wide_ref.shape[1]
    cols = pl.ds(pl.multiple_of(m * rows, rows), rows)
    return [
        pltpu.make_async_copy(residual_hbm.at[:, cols], wide_ref, sems.at[0]),
        pltpu.make_async_copy(back_hbm.at[:, cols], back_ref, sems.at[1]),
    ]


def start_load(*args):
    for copy in load_copies(*args):
        copy.start()


def wait_load(*args):
    for copy in load_copies(*args):
        copy.wait()


def backward_inputs(lens, heads, inner, model, rows):
    whole = pl.BlockSpec(memory_space=pltpu.VMEM)
    anywhere = pl.BlockSpec(memory_space=pl.ANY)
    once = lambda shape: pl.BlockSpec(
        (1,) + shape, lambda m: (m,) + (0,) * len(shape), pipeline_mode=pl.Buffered(1)
    )
    return [
        pl.BlockSpec((1, 1, lens.shape[2]), lambda m: (m, 0, 0), memory_space=pltpu.SMEM),
        once((model, rows)),
        once((model, rows)),
        anywhere,
        anywhere,
        once((3 * inner, rows)),
        once((inner, rows)),
        once((heads, 8, rows)),
        whole,
        whole,
        whole,
        whole,
        whole,
    ]


def backward_scratch(heads, inner, model, rows, wide):
    diag_count = 2 * (rows // tile) - 1
    return [
        pltpu.VMEM((wide, rows), f32),
        pltpu.VMEM((wide, rows), f32),
        pltpu.VMEM((heads, diag_count, tile, tile), bf16),
        pltpu.VMEM((heads, diag_count, tile, tile), f32),
        pltpu.VMEM((model, rows), bf16),
        pltpu.VMEM((3 * inner, rows), bf16),
        pltpu.VMEM((2, model, tile), f32),
        pltpu.SemaphoreType.DMA((2,)),
    ]


def attention_backward(
    lens, tok, og, residual, back, qkv, attended, log_total, qkv_w, out_w, gains, table, bucket,
    shard_rows, pad_rows,
):
    micro, model, rows = tok.shape
    inner = out_w.shape[1]
    heads = log_total.shape[1]
    wide = back.shape[0]
    whole = pl.BlockSpec(memory_space=pltpu.VMEM)
    return pl.pallas_call(
        functools.partial(attention_backward_kernel, shard_rows=shard_rows, pad_rows=pad_rows),
        grid=(micro,),
        in_specs=backward_inputs(lens, heads, inner, model, rows),
        out_specs=[pl.BlockSpec((1, model, rows), lambda m: (m, 0, 0))] + [whole] * 4,
        out_shape=[
            jax.ShapeDtypeStruct((micro, model, rows), bf16),
            jax.ShapeDtypeStruct((model, 3 * inner), f32),
            jax.ShapeDtypeStruct((model, inner), f32),
            jax.ShapeDtypeStruct((table.shape[0], table.shape[1]), f32),
            jax.ShapeDtypeStruct((16, model), f32),
        ],
        scratch_shapes=backward_scratch(heads, inner, model, rows, wide),
        compiler_params=pltpu.CompilerParams(vmem_limit_bytes=vmem_bytes),
        name="attention_backward",
    )(lens, tok, og, residual, back, qkv, attended, log_total, qkv_w, out_w, gains, table, bucket)


class Place:
    def __init__(self, row_count):
        self.row_count = row_count
        self.y = lax.axis_index("dp")
        self.z = lax.axis_index("row")
        col = lax.axis_index("col")
        self.x = col // 2
        self.core = col % 2
        self.near_x = self.x + (1 - self.core) * (1 - 2 * self.x)
        self.near_y = self.y + self.core * (1 - 2 * self.y)
        self.far_x = self.x + self.core * (1 - 2 * self.x)
        self.far_y = self.y + (1 - self.core) * (1 - 2 * self.y)

    def at(self, x, y, z, core):
        return (y, z, 2 * x + core)

    def near(self):
        return self.at(self.near_x, self.near_y, self.z, self.core)

    def far(self):
        return self.at(self.far_x, self.far_y, self.z, self.core)

    def partner(self):
        return self.at(self.x, self.y, self.z, 1 - self.core)

    def beside_y(self):
        return self.at(self.x, 1 - self.y, self.z, self.core)

    def beside_x(self):
        return self.at(1 - self.x, self.y, self.z, self.core)

    def along(self, step):
        return self.at(self.x, self.y, lax.rem(self.z + step, self.row_count), self.core)

    def greet(self, across=False):
        barrier = pltpu.get_barrier_semaphore()
        others = [self.near(), self.far(), self.partner()]
        for step in range(1, self.row_count):
            others.append(self.along(step))
            if across:
                z = lax.rem(self.z + step, self.row_count)
                others.append(self.at(1 - self.x, self.y, z, self.core))
        for other in others:
            pl.semaphore_signal(barrier, inc=1, device_id=other, device_id_type=MESH)
        pl.semaphore_wait(barrier, len(others))


def send(source, target, send_sem, recv_sem, device):
    return pltpu.make_async_remote_copy(
        src_ref=source,
        dst_ref=target,
        send_sem=send_sem,
        recv_sem=recv_sem,
        device_id=device,
        device_id_type=MESH,
    )


def gather_semaphores(steps, row_count):
    dma = pltpu.SemaphoreType.DMA
    return [
        dma((steps,)),
        dma((2, steps, row_count - 1)),
        dma((2, steps, 3)),
        dma((2, steps, 4)),
    ]


class Gather:
    def __init__(self, place, shard_ref, full_ref, sems, base=0):
        self.place, self.shard, self.full, self.base = place, shard_ref, full_ref, base
        self.local, self.line, self.cross, self.pair = sems
        self.pad_rows = shard_ref.shape[2]
        self.unit_rows = self.pad_rows * place.row_count

    def unit(self, t, x, y, core):
        rows = pl.ds(pl.multiple_of(y * self.unit_rows, self.unit_rows), self.unit_rows)
        return self.full.at[t - self.base, 2 * x + core, :, rows, :]

    def own(self, t):
        p = self.place
        index = p.y * p.row_count + p.z
        rows = pl.ds(pl.multiple_of(index * self.pad_rows, self.pad_rows), self.pad_rows)
        return self.full.at[t - self.base, 2 * p.x + p.core, :, rows, :]

    def copy_local(self, t):
        return pltpu.make_async_copy(self.shard.at[t], self.own(t), self.local.at[t])

    def copy_line(self, t, step):
        return send(
            self.shard.at[t],
            self.own(t),
            self.line.at[0, t, step - 1],
            self.line.at[1, t, step - 1],
            self.place.along(step),
        )

    def copy_cross(self, t, which):
        p = self.place
        x, y = ((p.x, p.y), (p.x, p.y), (p.near_x, p.near_y))[which]
        unit = self.unit(t, x, y, p.core)
        device = p.near() if which == 0 else p.far()
        return send(unit, unit, self.cross.at[0, t, which], self.cross.at[1, t, which], device)

    def copy_pair(self, t, which):
        p = self.place
        x, y = (
            (p.x, p.y),
            (p.near_x, p.near_y),
            (p.far_x, p.far_y),
            (1 - p.x, 1 - p.y),
        )[which]
        unit = self.unit(t, x, y, p.core)
        return send(
            unit, unit, self.pair.at[0, t, which], self.pair.at[1, t, which], p.partner()
        )

    def begin(self, t):
        self.copy_local(t).start()
        for step in range(1, self.place.row_count):
            self.copy_line(t, step).start()

    def spread(self, t):
        self.copy_local(t).wait()
        for step in range(1, self.place.row_count):
            self.copy_line(t, step).wait_recv()
        self.copy_cross(t, 0).start()
        self.copy_cross(t, 1).start()
        self.copy_pair(t, 0).start()

    def relay(self, t):
        self.copy_cross(t, 0).wait_recv()
        self.copy_cross(t, 2).start()
        self.copy_pair(t, 1).start()
        self.copy_cross(t, 1).wait_recv()
        self.copy_pair(t, 2).start()

    def settle(self, t):
        self.copy_cross(t, 2).wait_recv()
        self.copy_pair(t, 3).start()

    def finish(self, t):
        for which in range(4):
            self.copy_pair(t, which).wait_recv()

    def drain(self, t):
        for step in range(1, self.place.row_count):
            self.copy_line(t, step).wait_send()
        for which in range(3):
            self.copy_cross(t, which).wait_send()
        for which in range(4):
            self.copy_pair(t, which).wait_send()


class Share:
    def __init__(self, place, pairs, sems):
        self.place, self.pairs, self.sems = place, pairs, sems

    def rows(self, ref, core):
        half = ref.shape[0] // 2
        return pl.ds(pl.multiple_of(core * half, half), half)

    def copy_local(self, i):
        own, full = self.pairs[i]
        return pltpu.make_async_copy(own, full.at[self.place.y], self.sems.at[0, i, 0])

    def copy_over(self, i):
        own, full = self.pairs[i]
        p = self.place
        rows = self.rows(own, p.core)
        return send(
            own.at[rows, :],
            full.at[p.y, rows, :],
            self.sems.at[0, i, 1],
            self.sems.at[1, i, 1],
            p.beside_y(),
        )

    def copy_pair(self, i):
        own, full = self.pairs[i]
        p = self.place
        part = full.at[1 - p.y, self.rows(own, p.core), :]
        return send(part, part, self.sems.at[0, i, 2], self.sems.at[1, i, 2], p.partner())

    def begin(self):
        for i in range(len(self.pairs)):
            self.copy_over(i).start()
        for i in range(len(self.pairs)):
            self.copy_local(i).start()

    def relay(self):
        for i in range(len(self.pairs)):
            self.copy_over(i).wait_recv()
            self.copy_pair(i).start()

    def finish(self):
        for i in range(len(self.pairs)):
            self.copy_local(i).wait()
            self.copy_pair(i).wait_recv()

    def drain(self):
        for i in range(len(self.pairs)):
            self.copy_over(i).wait_send()
            self.copy_pair(i).wait_send()


def add_into(into, other):
    into[...] = into[...] + other[...]


def tables_of(small_ref, table_rows, bucket_part):
    return [small_ref[y, 16 : 16 + table_rows, 0:bucket_part] for y in range(2)]


def fused_forward_kernel(
    lens_ref, tok_ref, og_ref, bucket_ref, shard_ref, qkv_own, out_own, small_own,
    normed_ref, normed_t_ref, og_pad_ref, og_pad_t_ref, qkv_ref, attended_ref, log_ref,
    residual_ref, full_ref, qkv_full, out_full, small_full, gains_full,
    tiles_ref, scaled_ref, gains_ref, qkv_w_ref, out_w_ref, small_ref,
    local, line, cross, pair, share_sems, keep_sems,
    *, row_count, shard_rows, pad_rows, table_rows, bucket_part,
):
    micro_index = pl.program_id(0)
    early = full_ref.shape[0]
    part = qkv_own.shape[0]
    place = Place(row_count)
    gather = Gather(place, shard_ref, full_ref, (local, line, cross, pair))
    share = Share(
        place,
        [(small_own, small_ref), (qkv_own, qkv_w_ref), (out_own, out_w_ref)],
        share_sems,
    )
    keeps = [
        pltpu.make_async_copy(source, target, keep_sems.at[i])
        for i, (source, target) in enumerate(
            (
                (qkv_w_ref, qkv_full),
                (out_w_ref, out_full),
                (small_ref, small_full),
                (gains_ref, gains_full),
            )
        )
    ]

    @pl.when(micro_index == 0)
    def _():
        place.greet()
        share.begin()
        for t in range(early):
            gather.begin(t)

    pad_cotangent(og_ref, og_pad_ref, og_pad_t_ref, shard_rows, pad_rows)

    @pl.when(micro_index == 0)
    def _():
        gather.spread(0)
        share.relay()
        for t in range(1, early):
            gather.spread(t)
        share.finish()
        for y in range(2):
            turned = small_ref[y, 0:16, :].astype(f32).T
            gains_ref[y * part : (y + 1) * part, :] = turned[:part, :]
        for keep in keeps:
            keep.start()
        fill_bias_tiles(tables_of(small_ref, table_rows, bucket_part), bucket_ref, tiles_ref)

    def between():
        @pl.when(micro_index == 0)
        def _():
            gather.relay(0)

        @pl.when(micro_index == 1)
        def _():
            gather.settle(0)

    attend(
        lens_ref, tok_ref, qkv_w_ref, out_w_ref, gains_ref, normed_ref, normed_t_ref, qkv_ref,
        attended_ref, log_ref, residual_ref, tiles_ref, scaled_ref, shard_rows, pad_rows, between,
    )

    @pl.when(micro_index == 0)
    def _():
        for t in range(1, early):
            gather.relay(t)

    @pl.when(micro_index == 1)
    def _():
        for t in range(1, early):
            gather.settle(t)
        share.drain()
        for keep in keeps:
            keep.wait()
        for t in range(early):
            gather.finish(t)
            gather.drain(t)


def fused_forward(
    lens, tok, og, bucket, shard, qkv_w, out_w, small, heads, early, shard_rows, pad_rows,
    row_count, col_count, bucket_part,
):
    micro, model, rows = tok.shape
    inner = out_w.shape[1]
    steps, kinds = shard.shape[:2]
    wide = model // shard_rows * pad_rows
    anywhere = pl.BlockSpec(memory_space=pl.ANY)
    whole = pl.BlockSpec(memory_space=pltpu.VMEM)
    once = lambda shape: pl.BlockSpec((1,) + shape, lambda m: (m,) + (0,) * len(shape))
    double = lambda a: jax.ShapeDtypeStruct((2,) + a.shape, a.dtype)
    out_specs, out_shape = forward_outputs(micro, heads, inner, model, rows, wide)
    dma = pltpu.SemaphoreType.DMA
    return pl.pallas_call(
        functools.partial(
            fused_forward_kernel, row_count=row_count, shard_rows=shard_rows, pad_rows=pad_rows,
            table_rows=16, bucket_part=bucket_part,
        ),
        grid=(micro,),
        in_specs=[
            pl.BlockSpec((1, 1, lens.shape[2]), lambda m: (m, 0, 0), memory_space=pltpu.SMEM),
            once((model, rows)),
            once((model, rows)),
            whole,
        ]
        + [anywhere] * 4,
        out_specs=out_specs + [anywhere] * 5,
        out_shape=out_shape
        + [
            jax.ShapeDtypeStruct((early, col_count, kinds, wide, tile), bf16),
            double(qkv_w),
            double(out_w),
            double(small),
            jax.ShapeDtypeStruct((model, 16), f32),
        ],
        scratch_shapes=[
            pltpu.VMEM((heads, 2 * (rows // tile) - 1, tile, tile), bf16),
            pltpu.VMEM((model, rows), f32),
            pltpu.VMEM((model, 16), f32),
            pltpu.VMEM((2,) + qkv_w.shape, bf16),
            pltpu.VMEM((2,) + out_w.shape, bf16),
            pltpu.VMEM((2,) + small.shape, bf16),
        ]
        + gather_semaphores(steps, row_count)
        + [dma((2, 3, 3)), dma((4,))],
        compiler_params=pltpu.CompilerParams(
            collective_id=0, has_side_effects=True, vmem_limit_bytes=vmem_bytes
        ),
        name="fused_forward",
    )(lens, tok, og, bucket, shard, qkv_w, out_w, small)


def fused_hidden_kernel(
    normed_hbm, normed_t_hbm, og_hbm, og_t_hbm, residual_hbm, first_ref, shard_ref,
    layer_hbm, back_hbm, sums_hbm, rest_ref, landed_hbm,
    normed_ref, normed_t_ref, og_ref, og_t_ref, branch_ref, back_ref, hidden_ref, gate_ref, up_ref,
    weight_ref, grad_ref, other_ref, layer_ref,
    local, line, cross, pair, load_sems, weight_sems, store_sems, swap_sems, far_sems,
    credit,
    *, row_count, shard_rows, pad_rows,
):
    t = pl.program_id(0)
    steps, col_count = shard_ref.shape[0], weight_ref.shape[1]
    early = first_ref.shape[0]
    tokens, wide = normed_ref.shape
    place = Place(row_count)
    slot = lax.rem(t, 2)
    gather = Gather(place, shard_ref, rest_ref, (local, line, cross, pair), early)
    reduce = Reduce(place, sums_hbm, landed_hbm, far_sems)
    ahead = landed_hbm.shape[0]

    def load_early(q):
        s = lax.rem(q, 2)
        return pltpu.make_async_copy(first_ref.at[q], weight_ref.at[s], weight_sems.at[s])

    def load_late(q):
        s = lax.rem(q, 2)
        return pltpu.make_async_copy(rest_ref.at[q - early], weight_ref.at[s], weight_sems.at[s])

    def swap(q):
        s = lax.rem(q, 2)
        return send(
            grad_ref.at[s, :, 1 - place.core], other_ref.at[s], swap_sems.at[0, q],
            swap_sems.at[1, q], place.partner(),
        )

    def store(q):
        s = lax.rem(q, 2)
        return pltpu.make_async_copy(
            grad_ref.at[s, :, place.core], sums_hbm.at[q], store_sems.at[s]
        )

    def fold(q):
        s = lax.rem(q, 2)
        swap(q).wait_recv()
        for x in range(col_count // 2):
            for kind in range(3):
                add_into(grad_ref.at[s, x, place.core, kind], other_ref.at[s, x, kind])
        store(q).start()

        @pl.when(q < steps - 2)
        def _():
            pl.semaphore_signal(credit, 1, device_id=place.partner(), device_id_type=MESH)

    def late(q):
        return (q >= early) & (q < steps)

    @pl.when(t == 0)
    def _():
        loads = [
            pltpu.make_async_copy(source, target, load_sems.at[i])
            for i, (source, target) in enumerate(
                (
                    (normed_hbm, normed_ref),
                    (og_hbm, og_ref),
                    (normed_t_hbm, normed_t_ref),
                    (og_t_hbm, og_t_ref),
                    (residual_hbm, branch_ref),
                )
            )
        ]
        load_early(0).start()
        for load in loads:
            load.start()
        place.greet()
        for q in range(early, steps):
            gather.begin(q)
        back_ref[...] = jnp.zeros(back_ref.shape, f32)
        for load in loads:
            load.wait()
        for q in range(early, 4):
            gather.spread(q)

    @pl.when(t < early)
    def _():
        load_early(t).wait()

    @pl.when(t >= early)
    def _():
        load_late(t).wait()

    weights_now = weight_ref.at[slot]
    matrices = [[weights_now.at[j, which] for j in range(col_count)] for which in range(3)]
    unit = Hidden(
        matrices, normed_ref, normed_t_ref, og_ref, og_t_ref, branch_ref, back_ref, hidden_ref,
        gate_ref, up_ref, lambda which, j: grad_ref.at[slot, j // 2, j % 2, which],
    )
    unit.project(0, tokens // unit.block)

    @pl.when(t >= 1)
    def _():
        fold(t - 1)

    @pl.when(t >= 2)
    def _():
        swap(t - 2).wait_send()
        store(t - 2).wait()

    def send_far(step, chunks):
        @pl.when(t == step)
        def _():
            for q in chunks:
                reduce.begin(q)

    send_far(steps - 2, [2])
    send_far(steps - 1, [4])

    spans = wide // unit.span
    unit.weights(0, spans - 1)

    @pl.when(late(t + 2))
    def _():
        gather.relay(t + 2)

    @pl.when(late(t + 4))
    def _():
        gather.spread(t + 4)

    @pl.when(late(t + 1))
    def _():
        gather.settle(t + 1)

    @pl.when(t + 1 < early)
    def _():
        load_early(t + 1).start()

    send_far(steps - 3, [0, 1])
    send_far(steps - 2, [3])

    unit.weights(spans - 1, spans)

    @pl.when(late(t + 1))
    def _():
        gather.finish(t + 1)
        load_late(t + 1).start()

    @pl.when(t >= 2)
    def _():
        pl.semaphore_wait(credit, 1)

    swap(t).start()

    @pl.when(t == steps - 1)
    def _():
        out = pltpu.make_async_copy(back_ref, back_hbm, load_sems.at[0])
        out.start()
        rows = layer_ref.shape[1]
        for m in range(tokens // rows):
            for k in range(wide // pad_rows):
                source = slice(k * pad_rows, k * pad_rows + shard_rows)
                part = slice(k * shard_rows, (k + 1) * shard_rows)
                layer_ref[part, :] = branch_ref[source, m * rows : (m + 1) * rows].astype(bf16)
            layer_out = pltpu.make_async_copy(layer_ref, layer_hbm.at[m], load_sems.at[1])
            layer_out.start()
            layer_out.wait()
        fold(t)
        swap(t - 1).wait_send()
        swap(t).wait_send()
        store(t - 1).wait()
        store(t).wait()
        out.wait()
        for q in range(early, steps):
            gather.drain(q)
        for q in range(ahead):
            for which in range(2):
                reduce.copy_far(q, which).wait()


def fused_hidden(
    normed, normed_t, og, og_t, residual, first, shard, micro, model, shard_rows, pad_rows,
    row_count, ahead,
):
    tokens, wide = normed.shape
    rows = tokens // micro
    steps, kinds = shard.shape[:2]
    early, col_count = first.shape[:2]
    x_count = col_count // 2
    width = col_count * tile
    anywhere = pl.BlockSpec(memory_space=pl.ANY)
    dma = pltpu.SemaphoreType.DMA
    return pl.pallas_call(
        functools.partial(
            fused_hidden_kernel, row_count=row_count, shard_rows=shard_rows, pad_rows=pad_rows
        ),
        grid=(steps,),
        in_specs=[anywhere] * 7,
        out_specs=[anywhere] * 5,
        out_shape=[
            jax.ShapeDtypeStruct((micro, model, rows), bf16),
            jax.ShapeDtypeStruct((wide, tokens), f32),
            jax.ShapeDtypeStruct((steps, x_count, kinds, wide, tile), bf16),
            jax.ShapeDtypeStruct((steps - early,) + first.shape[1:], bf16),
            jax.ShapeDtypeStruct((ahead, 2, kinds, pad_rows * row_count, tile), bf16),
        ],
        scratch_shapes=[
            pltpu.VMEM((tokens, wide), bf16),
            pltpu.VMEM((wide, tokens), bf16),
            pltpu.VMEM((tokens, wide), bf16),
            pltpu.VMEM((wide, tokens), bf16),
            pltpu.VMEM((wide, tokens), f32),
            pltpu.VMEM((wide, tokens), f32),
            pltpu.VMEM((tokens, width), bf16),
            pltpu.VMEM((tokens, width), bf16),
            pltpu.VMEM((tokens, width), bf16),
            pltpu.VMEM((2, col_count, kinds, wide, tile), bf16),
            pltpu.VMEM((2, x_count, 2, kinds, wide, tile), bf16),
            pltpu.VMEM((2, x_count, kinds, wide, tile), bf16),
            pltpu.VMEM((model, rows), bf16),
        ]
        + gather_semaphores(steps, row_count)
        + [
            dma((5,)),
            dma((2,)),
            dma((2,)),
            dma((2, steps)),
            dma((2, ahead, 2)),
            pltpu.SemaphoreType.REGULAR,
        ],
        compiler_params=pltpu.CompilerParams(
            collective_id=1, has_side_effects=True, vmem_limit_bytes=vmem_bytes
        ),
        name="fused_hidden",
    )(normed, normed_t, og, og_t, residual, first, shard)


class Reduce:
    slots = 2

    def __init__(
        self, place, source, second, cross, landed=None, landed_sems=None, stage=None, third=None,
        fourth=None, load=None, line=None,
    ):
        self.place, self.source, self.second, self.cross = place, source, second, cross
        self.landed, self.landed_sems, self.stage = landed, landed_sems, stage
        self.third, self.fourth, self.load, self.line = third, fourth, load, line
        self.unit_rows = second.shape[3]
        self.pad_rows = self.unit_rows // place.row_count
        self.ahead = 0 if landed is None else landed.shape[0]

    def unit(self, t, x, y):
        rows = pl.ds(pl.multiple_of(y * self.unit_rows, self.unit_rows), self.unit_rows)
        return self.source.at[t, x, :, rows, :]

    def shard(self, row):
        return pl.ds(pl.multiple_of(row * self.pad_rows, self.pad_rows), self.pad_rows)

    def copy_own(self, t, which):
        p = self.place
        slot = t % self.slots
        x, y = ((p.x, p.y), (p.near_x, p.near_y))[which]
        return pltpu.make_async_copy(
            self.unit(t, x, y), self.stage.at[slot, which], self.load.at[slot, which]
        )

    def copy_far(self, t, which):
        p = self.place
        x, y = ((p.far_x, p.far_y), (1 - p.x, 1 - p.y))[which]
        return send(
            self.unit(t, x, y), self.second.at[t, which], self.cross.at[0, t, which],
            self.cross.at[1, t, which], p.far(),
        )

    def copy_near(self, t):
        return send(
            self.second.at[t, 1], self.third.at[t], self.cross.at[0, t, 2],
            self.cross.at[1, t, 2], self.place.near(),
        )

    def copy_line(self, t, step):
        p = self.place
        rows = self.shard(lax.rem(p.z + step, p.row_count))
        return send(
            self.second.at[t, 0, :, rows, :], self.fourth.at[t, step - 1],
            self.line.at[0, t, step - 1], self.line.at[1, t, step - 1], p.along(step),
        )

    def copy_landed(self, t):
        return pltpu.make_async_copy(
            self.landed.at[t], self.second.at[t], self.landed_sems.at[t]
        )

    def load_own(self, t):
        for which in range(2):
            self.copy_own(t, which).start()

    def begin(self, t):
        self.copy_far(t, 1).start()
        self.copy_far(t, 0).start()

    def fold_far(self, t):
        self.copy_own(t, 1).wait()
        if t < self.ahead:
            self.copy_landed(t).wait()
        else:
            self.copy_far(t, 1).wait_recv()
        slot = t % self.slots
        for kind in range(3):
            add_into(self.second.at[t, 1, kind], self.stage.at[slot, 1, kind])
        self.copy_near(t).start()
        self.copy_own(t, 0).wait()
        if t >= self.ahead:
            self.copy_far(t, 0).wait_recv()
        for kind in range(3):
            add_into(self.second.at[t, 0, kind], self.stage.at[slot, 0, kind])

    def fold_near(self, t):
        self.copy_near(t).wait_recv()
        for kind in range(3):
            add_into(self.second.at[t, 0, kind], self.third.at[t, kind])
        for step in range(1, self.place.row_count):
            self.copy_line(t, step).start()

    def total(self, t, kind):
        total = self.second[t, 0, kind, self.shard(self.place.z), :].astype(f32)
        for step in range(1, self.place.row_count):
            total = total + self.fourth[t, step - 1, kind].astype(f32)
        return total

    def wait_line(self, t):
        for step in range(1, self.place.row_count):
            self.copy_line(t, step).wait_recv()

    def drain(self, t):
        if t >= self.ahead:
            for which in range(2):
                self.copy_far(t, which).wait_send()
        self.copy_near(t).wait_send()
        for step in range(1, self.place.row_count):
            self.copy_line(t, step).wait_send()


class Dense:
    def __init__(self, place, source, first, second, third, piece, out, sems):
        self.place, self.source = place, source
        self.first, self.second, self.third, self.piece = first, second, third, piece
        self.out, self.sems = out, sems
        self.half = second.shape[0]
        self.piece_rows = piece.shape[0]
        self.offsets = [
            (dx, dz) for dx in range(2) for dz in range(place.row_count) if (dx, dz) != (0, 0)
        ]

    def rows(self, start, size):
        return pl.ds(pl.multiple_of(start, 16), size)

    def sem(self, i):
        return self.sems.at[0, i], self.sems.at[1, i]

    def half_rows(self, core):
        return self.rows(core * self.half, self.half)

    def piece_at(self, dx, dz):
        p = self.place
        x = p.x + dx * (1 - 2 * p.x)
        z = lax.rem(p.z + dz, p.row_count)
        start = p.core * self.half + (x * p.row_count + z) * self.piece_rows
        return self.rows(start, self.piece_rows)

    def other(self, dx, dz):
        p = self.place
        x = p.x + dx * (1 - 2 * p.x)
        return p.at(x, p.y, lax.rem(p.z + dz, p.row_count), p.core)

    def copy_pair(self):
        p = self.place
        return send(
            self.source.at[:, self.half_rows(1 - p.core), :], self.first, *self.sem(0), p.partner()
        )

    def copy_y(self):
        p = self.place
        part = self.source.at[1 - p.y, self.half_rows(p.core), :]
        return send(part, self.second, *self.sem(1), p.beside_y())

    def copy_piece(self, i):
        part = self.source.at[self.place.y, self.piece_at(*self.offsets[i]), :]
        return send(part, self.third.at[i], *self.sem(3 + i), self.other(*self.offsets[i]))

    def keep_piece(self):
        return pltpu.make_async_copy(
            self.piece, self.out.at[self.piece_at(0, 0), :], self.sems.at[0, 2]
        )

    def back_piece(self, i):
        part = self.out.at[self.piece_at(0, 0), :]
        index = 3 + len(self.offsets) + i
        return send(self.piece, part, *self.sem(index), self.other(*self.offsets[i]))

    def back_pair(self):
        p = self.place
        part = self.out.at[self.half_rows(p.core), :]
        return send(part, part, *self.sem(3 + 2 * len(self.offsets)), p.partner())

    def begin(self):
        self.copy_pair().start()

    def fold_pair(self):
        p = self.place
        self.copy_pair().wait_recv()
        rows = self.half_rows(p.core)
        add_into(self.source.at[1 - p.y, rows, :], self.first.at[1 - p.y])
        self.copy_y().start()
        add_into(self.source.at[p.y, rows, :], self.first.at[p.y])

    def fold_y(self):
        p = self.place
        self.copy_y().wait_recv()
        add_into(self.source.at[p.y, self.half_rows(p.core), :], self.second)
        for i in range(len(self.offsets)):
            self.copy_piece(i).start()

    def fold_pieces(self):
        for i in range(len(self.offsets)):
            self.copy_piece(i).wait_recv()
        total = self.source[self.place.y, self.piece_at(0, 0), :].astype(f32)
        for i in range(len(self.offsets)):
            total = total + self.third[i].astype(f32)
        self.piece[...] = total.astype(bf16)
        self.keep_piece().start()
        for i in range(len(self.offsets)):
            self.back_piece(i).start()

    def return_pair(self):
        self.keep_piece().wait()
        for i in range(len(self.offsets)):
            self.back_piece(i).wait_recv()
        self.back_pair().start()

    def finish(self):
        self.back_pair().wait_recv()
        self.copy_pair().wait_send()
        self.copy_y().wait_send()
        self.back_pair().wait_send()
        for i in range(len(self.offsets)):
            self.copy_piece(i).wait_send()
            self.back_piece(i).wait_send()


def fused_backward_kernel(
    lens_ref, tok_ref, og_ref, residual_hbm, back_hbm, qkv_ref, attended_ref, log_ref, qkv_w_ref,
    out_w_ref, gains_ref, small_ref, bucket_ref, source_ref, landed_ref,
    tok_grad_ref, inner_ref, outer_ref, dense_out,
    wide_ref, back_ref, tiles_ref, diag_ref, low_ref, grad_qkv_ref, fold_ref, load_sems,
    stage, second, third, fourth,
    dense_ref, dense_first, dense_second, dense_third, dense_piece,
    load, cross, line, landed_sems, dense_sems,
    *, row_count, shard_rows, pad_rows, bucket_part,
):
    micro_index = pl.program_id(0)
    model, rows = tok_ref.shape[1:]
    inner = attended_ref.shape[1]
    part = model // 2
    size = model // 4
    steps = source_ref.shape[0]
    place = Place(row_count)
    reduce = Reduce(
        place, source_ref, second, cross, landed_ref, landed_sems, stage, third, fourth, load, line
    )
    dense = Dense(
        place, dense_ref, dense_first, dense_second, dense_third, dense_piece, dense_out,
        dense_sems,
    )

    def finish_chunk(t):
        reduce.wait_line(t)
        lanes = slice(t * tile, (t + 1) * tile)
        for kind in range(2):
            inner_ref[kind, :, lanes] = reduce.total(t, kind)[:shard_rows]
        outer_ref[:, lanes] = reduce.total(t, 2)[:shard_rows]

    def group(n):
        if n < steps:
            reduce.fold_far(n)
            if n + reduce.slots < steps:
                reduce.load_own(n + reduce.slots)
        if 0 <= n - 1 < steps:
            reduce.fold_near(n - 1)
        if 0 <= n - 2 < steps:
            finish_chunk(n - 2)

    start_load(residual_hbm, back_hbm, wide_ref, back_ref, load_sems, micro_index)

    @pl.when(micro_index == 0)
    def _():
        for t in range(reduce.slots):
            reduce.load_own(t)
        for t in range(reduce.ahead):
            reduce.copy_landed(t).start()
        place.greet(True)
        group(0)
        fill_bias_tiles(tables_of(small_ref, 16, bucket_part), bucket_ref, tiles_ref)
        diag_ref[...] = jnp.zeros(diag_ref.shape, f32)
        fold_ref[...] = jnp.zeros(fold_ref.shape, f32)
        dense_ref[...] = jnp.zeros(dense_ref.shape, bf16)

    wait_load(residual_hbm, back_hbm, wide_ref, back_ref, load_sems, micro_index)

    def add(k, start, value):
        at = (k // 2, slice((k % 2) * size, (k % 2 + 1) * size), slice(start, start + value.shape[1]))
        dense_ref[at] = (dense_ref[at].astype(f32) + value).astype(bf16)

    def before_heads():
        @pl.when(micro_index == 0)
        def _():
            group(1)
            for t in range(reduce.ahead, steps):
                reduce.begin(t)

        @pl.when(micro_index == 1)
        def _():
            group(3)

    def after_heads():
        @pl.when(micro_index == 0)
        def _():
            group(2)

        @pl.when(micro_index == 1)
        def _():
            group(4)

    attend_back(
        lens_ref, tok_ref, og_ref, Padded(wide_ref, shard_rows, pad_rows),
        Padded(back_ref, shard_rows, pad_rows), qkv_ref, attended_ref, log_ref, qkv_w_ref,
        out_w_ref, gains_ref, tok_grad_ref, tiles_ref, diag_ref, low_ref, grad_qkv_ref, fold_ref,
        lambda k, value: add(k, 3 * inner, value), lambda k, value: add(k, 0, value),
        before_heads, after_heads,
    )

    @pl.when(micro_index == 1)
    def _():
        half = bucket_part
        sums = bucket_sums(diag_ref, bucket_ref, 2 * half, 16).astype(bf16)
        for y in range(2):
            gains = gain_rows_of(fold_ref, y * part, (y + 1) * part)
            dense_ref[y, part : part + 16, 0:part] = gains.astype(bf16)
            dense_ref[y, part + 16 : part + 32, 0:half] = sums[:, y * half : (y + 1) * half]
        dense.begin()
        group(5)
        dense.fold_pair()
        group(6)
        dense.fold_y()
        group(7)
        dense.fold_pieces()
        for n in range(8, steps + 2):
            group(n)
        dense.return_pair()
        dense.finish()
        for t in range(steps):
            reduce.drain(t)


def fused_backward(
    lens, tok, og, residual, back, qkv, attended, log_total, qkv_w, out_w, gains, small, bucket,
    source, landed, dense_rows, shard_rows, pad_rows, row_count, bucket_part,
):
    micro, model, rows = tok.shape
    inner = out_w.shape[1]
    heads = log_total.shape[1]
    steps, x_count, kinds, wide, _ = source.shape
    unit_rows = pad_rows * row_count
    slots = Reduce.slots
    width = 4 * inner
    half = dense_rows // 2
    piece_rows = half // (2 * row_count)
    hidden = steps * tile
    anywhere = pl.BlockSpec(memory_space=pl.ANY)
    inside = pl.BlockSpec(memory_space=pltpu.VMEM)
    dma = pltpu.SemaphoreType.DMA
    return pl.pallas_call(
        functools.partial(
            fused_backward_kernel, row_count=row_count, shard_rows=shard_rows, pad_rows=pad_rows,
            bucket_part=bucket_part,
        ),
        grid=(micro,),
        in_specs=backward_inputs(lens, heads, inner, model, rows) + [anywhere] * 2,
        out_specs=[
            pl.BlockSpec(
                (1, model, rows), lambda m: (m, 0, 0), pipeline_mode=pl.Buffered(1)
            ),
            inside,
            inside,
            anywhere,
        ],
        out_shape=[
            jax.ShapeDtypeStruct((micro, model, rows), bf16),
            jax.ShapeDtypeStruct((2, shard_rows, hidden), f32),
            jax.ShapeDtypeStruct((shard_rows, hidden), f32),
            jax.ShapeDtypeStruct((dense_rows, width), bf16),
        ],
        scratch_shapes=backward_scratch(heads, inner, model, rows, wide)
        + [
            pltpu.VMEM((slots, 2, kinds, unit_rows, tile), bf16),
            pltpu.VMEM((steps, 2, kinds, unit_rows, tile), bf16),
            pltpu.VMEM((steps, kinds, unit_rows, tile), bf16),
            pltpu.VMEM((steps, row_count - 1, kinds, pad_rows, tile), bf16),
            pltpu.VMEM((2, dense_rows, width), bf16),
            pltpu.VMEM((2, half, width), bf16),
            pltpu.VMEM((half, width), bf16),
            pltpu.VMEM((2 * row_count - 1, piece_rows, width), bf16),
            pltpu.VMEM((piece_rows, width), bf16),
            dma((slots, 2)),
            dma((2, steps, 3)),
            dma((2, steps, row_count - 1)),
            dma((landed.shape[0],)),
            dma((2, 4 + 2 * (2 * row_count - 1))),
        ],
        compiler_params=pltpu.CompilerParams(
            collective_id=2, has_side_effects=True, vmem_limit_bytes=vmem_bytes
        ),
        name="fused_backward",
    )(
        lens, tok, og, residual, back, qkv, attended, log_total, qkv_w, out_w, gains, small,
        bucket, source, landed,
    )


def round_up(value, multiple):
    return -(-value // multiple) * multiple


def shards(
    tokens,
    out_grad,
    lengths,
    offset_bucket,
    qkv_weight,
    out_weight,
    bias_table,
    norm_gains,
    inner_weight,
    outer_weight,
):
    dp_count, row_count, col_count = (lax.axis_size(a) for a in ("dp", "row", "col"))
    shard_count = dp_count * row_count
    micro, rows, model = tokens.shape
    shard_rows = inner_weight.shape[1]
    hidden = inner_weight.shape[2]
    steps = hidden // tile
    heads = bias_table.shape[1]
    bucket_part = bias_table.shape[0]
    bucket_count = bucket_part * dp_count
    inner = out_weight.shape[0]
    part = qkv_weight.shape[0]
    head_rows = 16
    direct = (
        dp_count == 2 and col_count == 4 and part % 32 == 0 and shard_rows % 8 == 0 and steps >= 7
        and micro == 2
    )

    group_rows = shard_rows if direct else model // 2
    pad_rows = round_up(group_rows, 16 if direct else 256)

    tok_t = jnp.transpose(tokens, (0, 2, 1))
    og_t = jnp.transpose(out_grad, (0, 2, 1))
    out_part = out_weight.T
    small_width = round_up(max(part, bucket_part), tile)
    gain_rows = 16
    small = jnp.concatenate(
        [
            jnp.pad(norm_gains, ((0, gain_rows - 2), (0, small_width - part))),
            jnp.pad(bias_table.T, ((0, head_rows - heads), (0, small_width - bucket_part))),
        ],
        axis=0,
    )
    bucket = jnp.pad(offset_bucket[::-1], (0, 1), constant_values=-1)[None, :]
    packed = jnp.stack([inner_weight[0], inner_weight[1], outer_weight.T])
    if direct:
        packed = jnp.pad(packed, ((0, 0), (0, pad_rows - shard_rows), (0, 0)))
        packed = packed.reshape(3, pad_rows, steps, tile).transpose(2, 0, 1, 3)
        (
            normed, normed_t, og_pad, og_pad_t, qkv, attended, log_total, residual, first,
            qkv_full, out_full, small_full, gains,
        ) = fused_forward(
            lengths, tok_t, og_t, bucket, packed, qkv_weight, out_part, small, heads,
            2, group_rows, pad_rows, row_count, col_count, bucket_part,
        )
    else:
        packed = packed.reshape(3, shard_rows, steps, tile).transpose(2, 0, 1, 3)
        weights = lax.all_gather(packed, ("dp", "row"), axis=2, tiled=True)
        weights = jnp.moveaxis(lax.all_gather(weights, "col", axis=0), 0, 1)
        weights = weights.reshape(steps, col_count, 3, 2, group_rows, tile)
        weights = jnp.pad(weights, ((0, 0),) * 4 + ((0, pad_rows - group_rows), (0, 0)))
        weights = weights.reshape(steps, col_count, 3, 2 * pad_rows, tile)
        qkv_full, out_full, small_full = (
            lax.all_gather(a, "dp", axis=0) for a in (qkv_weight, out_part, small)
        )
    qkv_full = qkv_full.reshape(1, model, 3 * inner)
    out_full = out_full.reshape(1, model, inner)
    if direct:
        layer_t, back, sums, _, landed = fused_hidden(
            normed, normed_t, og_pad, og_pad_t, residual, first, packed, micro, model, group_rows,
            pad_rows, row_count, 5,
        )
    else:
        gains = small_full[:, :2, :part].transpose(0, 2, 1).reshape(model, 2).astype(f32)
        table = small_full[:, gain_rows : gain_rows + head_rows, :bucket_part]
        table = table.transpose(1, 0, 2).reshape(head_rows, bucket_count)
        normed, normed_t, og_pad, og_pad_t, qkv, attended, log_total, residual = attention_forward(
            lengths, tok_t, og_t, qkv_full, out_full, gains, table, bucket, heads, group_rows,
            pad_rows,
        )
        layer_t, back, weight_grads = feed_forward(
            normed, normed_t, og_pad, og_pad_t, residual, weights, micro, model, group_rows,
            pad_rows,
        )
    qkv_full, out_full = qkv_full[0], out_full[0]
    backward = (
        lengths, tok_t, og_t, residual, back, qkv, attended, log_total, qkv_full, out_full, gains,
    )
    dense_rows = round_up(part + 32, 64 * row_count)
    if direct:
        tok_grad_t, inner_grad, outer_grad, total = fused_backward(
            *backward, small_full, bucket, sums, landed, dense_rows, group_rows, pad_rows, row_count,
            bucket_part,
        )
    else:
        tok_grad_t, qkv_grad, out_grads, table_grad, gains_grad = attention_backward(
            *backward, table, bucket, group_rows, pad_rows
        )
        width = 4 * inner
        table_part = table_grad.reshape(head_rows, dp_count, bucket_part).transpose(1, 0, 2)
        gains_part = gains_grad.reshape(16, dp_count, part).transpose(1, 0, 2)
        rest = dense_rows - part - 32
        dense = jnp.concatenate([qkv_grad, out_grads], axis=1).reshape(dp_count, part, width)
        dense = jnp.concatenate(
            [
                dense,
                jnp.pad(gains_part, ((0, 0), (0, 0), (0, width - part))),
                jnp.pad(table_part, ((0, 0), (0, rest), (0, width - bucket_part))),
            ],
            axis=1,
        ).astype(bf16)
        grads = weight_grads.reshape(steps, col_count, 3, 2, pad_rows, tile)
        grads = grads[:, :, :, :, :group_rows].reshape(steps, col_count, 3, model, tile)
        grads = jnp.moveaxis(grads, 1, 0)
        grads = lax.psum_scatter(grads, "col", scatter_dimension=0)
        grads = lax.psum_scatter(grads, ("dp", "row"), scatter_dimension=2, tiled=True)
        grads = grads.transpose(1, 2, 0, 3).reshape(3, shard_rows, hidden)
        inner_grad, outer_grad = grads[:2].astype(f32), grads[2].astype(f32)
        total = lax.psum_scatter(dense, "dp", scatter_dimension=0)
        total = lax.psum(total, ("row", "col"))
    total = total.astype(f32)
    return (
        jnp.transpose(layer_t, (0, 2, 1)),
        jnp.transpose(tok_grad_t, (0, 2, 1)),
        total[:part, : 3 * inner],
        total[:part, 3 * inner :].T,
        total[part + 16 : part + 16 + heads, :bucket_part].T,
        total[part : part + 2, :part],
        inner_grad,
        outer_grad.T,
    )


def solution(mesh):
    return jax.shard_map(
        shards,
        mesh=mesh,
        in_specs=(
            P(None, ("dp", "row", "col"), None),
            P(None, ("dp", "row", "col"), None),
            P(None, ("dp", "row", "col"), None),
            P(),
            P("dp", None),
            P(None, "dp"),
            P("dp", None),
            P(None, "dp"),
            P(None, ("dp", "row"), "col"),
            P("col", ("dp", "row")),
        ),
        out_specs=(
            P(None, ("dp", "row", "col"), None),
            P(None, ("dp", "row", "col"), None),
            P("dp", None),
            P(None, "dp"),
            P("dp", None),
            P(None, "dp"),
            P(None, ("dp", "row"), "col"),
            P("col", ("dp", "row")),
        ),
        check_vma=False,
    )
```

```python
import functools

import jax
import jax.numpy as jnp
from jax import lax
from jax.experimental import pallas as pl
from jax.experimental.pallas import tpu as pltpu
from jax.sharding import PartitionSpec as P

epsilon = 1e-06
masked_score = -1000000000.0
highest = lax.Precision.HIGHEST
gelu_scale = 0.7978845608028654
gelu_cubic = 0.044715
MESH = pl.DeviceIdType.MESH
f32 = jnp.float32
bf16 = jnp.bfloat16
tile = 128
vmem_bytes = 63 * 1024 * 1024


def dot_nn(a, b):
    return lax.dot_general(a, b, (((1,), (0,)), ((), ())), preferred_element_type=f32)


def dot_nt(a, b):
    return lax.dot_general(a, b, (((1,), (1,)), ((), ())), preferred_element_type=f32)


def dot_tn(a, b):
    return lax.dot_general(a, b, (((0,), (0,)), ((), ())), preferred_element_type=f32)


def bucket_onehot(bucket_ref, bucket_count):
    span = bucket_ref.shape[1]
    ids = lax.broadcasted_iota(jnp.int32, (bucket_count, span), 0)
    return ids == jnp.broadcast_to(bucket_ref[0:1, :], (bucket_count, span))


def fill_bias_tiles(tables, bucket_ref, tiles_ref):
    head_count, diag_count = tiles_ref.shape[:2]
    bucket_count = sum(table.shape[1] for table in tables)
    onehot = bucket_onehot(bucket_ref, bucket_count).astype(f32)
    rev = None
    start = 0
    for table in tables:
        stop = start + table.shape[1]
        part = dot_nn(table, onehot[start:stop].astype(bf16))
        rev = part if rev is None else rev + part
        start = stop
    for h in range(head_count):
        for d in range(diag_count):
            row = rev[h : h + 1, tile * d : tile * d + 2 * tile]
            wide = jnp.broadcast_to(row, (tile, 2 * tile))
            turned = pltpu.roll(wide, tile + 1, 1, stride=1, stride_axis=0)[:, :tile]
            tiles_ref[h, d] = turned.astype(tiles_ref.dtype)


def bias_block(tiles_ref, h, key_block, blocks):
    return jnp.concatenate(
        [tiles_ref[h, q - key_block + blocks - 1] for q in range(blocks)], axis=1
    )


def doc_labels(lens_ref, axis, rows):
    shape = (rows, 1) if axis == 0 else (1, rows)
    place = lax.broadcasted_iota(jnp.int32, shape, axis)
    label = jnp.zeros(shape, jnp.int32)
    end = jnp.int32(0)
    for slot in range(lens_ref.shape[2]):
        end = end + lens_ref[0, 0, slot]
        label = label + (place >= end).astype(jnp.int32)
    return label


def masked_scores(key_rows, query_cols, tiles_ref, h, same_doc, blocks):
    raw = dot_nn(key_rows, query_cols)
    bias = jnp.concatenate([bias_block(tiles_ref, h, kb, blocks) for kb in range(blocks)], axis=0)
    return jnp.where(same_doc, raw + bias.astype(f32), masked_score)


def pad_cotangent(og_ref, og_pad_ref, og_pad_t_ref, shard_rows, pad_rows):
    model, rows = og_ref.shape[1:]
    for k in range(model // shard_rows):
        part = slice(k * shard_rows, (k + 1) * shard_rows)
        og_pad_t_ref[k * pad_rows : k * pad_rows + shard_rows, :] = (
            og_ref[0, part, :].astype(f32).astype(bf16)
        )
        rest = slice(k * pad_rows + shard_rows, (k + 1) * pad_rows)
        if pad_rows > shard_rows:
            og_pad_t_ref[rest, :] = jnp.zeros((pad_rows - shard_rows, rows), bf16)
    og_pad_ref[...] = og_pad_t_ref[...].T


def attend(
    lens_ref,
    tok_ref,
    qkv_w_ref,
    out_w_ref,
    gains_ref,
    normed_ref,
    normed_t_ref,
    qkv_ref,
    attended_ref,
    log_ref,
    residual_ref,
    tiles_ref,
    scaled_ref,
    shard_rows,
    pad_rows,
    between,
):
    model, rows = tok_ref.shape[1:]
    inner = attended_ref.shape[1]
    head_count = tiles_ref.shape[0]
    head_dim = inner // head_count
    blocks = rows // tile
    parts = model // shard_rows
    slabs, slab_rows = qkv_w_ref.shape[:2]

    square = jnp.zeros((1, rows), f32)
    for k in range(parts):
        x = tok_ref[0, k * shard_rows : (k + 1) * shard_rows, :].astype(f32)
        square = square + jnp.sum(x * x, axis=0, keepdims=True)
    scale = lax.rsqrt(square / model + epsilon)
    for k in range(parts):
        part = slice(k * shard_rows, (k + 1) * shard_rows)
        x = tok_ref[0, part, :].astype(f32)
        scaled_ref[part, :] = x * scale * gains_ref[part, 0:1]
    total = None
    for slab in range(slabs):
        normed = scaled_ref[slab * slab_rows : (slab + 1) * slab_rows, :].astype(bf16)
        product = dot_tn(qkv_w_ref[slab], normed)
        total = product if total is None else total + product
    qkv_ref[0] = total.astype(bf16)

    same_doc = doc_labels(lens_ref, 0, rows) == doc_labels(lens_ref, 1, rows)

    def head(h, carry):
        base = pl.multiple_of(h * head_dim, head_dim)
        query_cols = qkv_ref[0, pl.ds(base, head_dim), :]
        key_cols = qkv_ref[0, pl.ds(inner + base, head_dim), :]
        value_cols = qkv_ref[0, pl.ds(2 * inner + base, head_dim), :]
        scores = masked_scores(key_cols.T, query_cols, tiles_ref, h, same_doc, blocks)
        peak = jnp.max(scores, axis=0, keepdims=True)
        weight = jnp.exp(scores - peak)
        total = jnp.sum(weight, axis=0, keepdims=True)
        low = (weight * (1.0 / total)).astype(bf16)
        attended_ref[0, pl.ds(base, head_dim), :] = dot_nn(value_cols, low).astype(bf16)
        log_ref[0, h] = jnp.broadcast_to(peak + jnp.log(total), (8, rows))
        return carry

    lax.fori_loop(0, head_count, head, 0)
    between()

    for slab in range(slabs):
        scaled_ref[slab * slab_rows : (slab + 1) * slab_rows, :] = dot_nn(
            out_w_ref[slab], attended_ref[0]
        )
    square = jnp.zeros((1, rows), f32)
    for k in range(parts):
        part = slice(k * shard_rows, (k + 1) * shard_rows)
        x = scaled_ref[part, :] + tok_ref[0, part, :].astype(f32)
        residual_ref[k * pad_rows : k * pad_rows + shard_rows, :] = x
        square = square + jnp.sum(x * x, axis=0, keepdims=True)
    scale = lax.rsqrt(square / model + epsilon)
    for k in range(parts):
        part = slice(k * shard_rows, (k + 1) * shard_rows)
        dest = slice(k * pad_rows, k * pad_rows + shard_rows)
        rest = slice(k * pad_rows + shard_rows, (k + 1) * pad_rows)
        x = residual_ref[dest, :]
        normed_t_ref[dest, :] = (x * scale * gains_ref[part, 1:2]).astype(bf16)
        if pad_rows > shard_rows:
            normed_t_ref[rest, :] = jnp.zeros((pad_rows - shard_rows, rows), bf16)
            residual_ref[rest, :] = jnp.zeros((pad_rows - shard_rows, rows), f32)
    normed_ref[...] = normed_t_ref[...].T


def attention_forward_kernel(
    lens_ref,
    tok_ref,
    og_ref,
    qkv_w_ref,
    out_w_ref,
    gains_ref,
    table_ref,
    bucket_ref,
    normed_ref,
    normed_t_ref,
    og_pad_ref,
    og_pad_t_ref,
    qkv_ref,
    attended_ref,
    log_ref,
    residual_ref,
    tiles_ref,
    scaled_ref,
    *,
    shard_rows,
    pad_rows,
):
    @pl.when(pl.program_id(0) == 0)
    def _():
        fill_bias_tiles([table_ref[...]], bucket_ref, tiles_ref)

    pad_cotangent(og_ref, og_pad_ref, og_pad_t_ref, shard_rows, pad_rows)
    attend(
        lens_ref, tok_ref, qkv_w_ref, out_w_ref, gains_ref, normed_ref, normed_t_ref, qkv_ref,
        attended_ref, log_ref, residual_ref, tiles_ref, scaled_ref, shard_rows, pad_rows,
        lambda: None,
    )


def forward_outputs(micro, heads, inner, model, rows, wide):
    once = lambda shape: pl.BlockSpec((1,) + shape, lambda m: (m,) + (0,) * len(shape))
    tokens = micro * rows
    across = pl.BlockSpec((rows, wide), lambda m: (m, 0))
    along = pl.BlockSpec((wide, rows), lambda m: (0, m))
    specs = [
        across, along, across, along, once((3 * inner, rows)), once((inner, rows)),
        once((heads, 8, rows)), along,
    ]
    shapes = [
        jax.ShapeDtypeStruct((tokens, wide), bf16),
        jax.ShapeDtypeStruct((wide, tokens), bf16),
        jax.ShapeDtypeStruct((tokens, wide), bf16),
        jax.ShapeDtypeStruct((wide, tokens), bf16),
        jax.ShapeDtypeStruct((micro, 3 * inner, rows), bf16),
        jax.ShapeDtypeStruct((micro, inner, rows), bf16),
        jax.ShapeDtypeStruct((micro, heads, 8, rows), f32),
        jax.ShapeDtypeStruct((wide, tokens), f32),
    ]
    return specs, shapes


def attention_forward(
    lens, tok, og, qkv_w, out_w, gains, table, bucket, heads, shard_rows, pad_rows
):
    micro, model, rows = tok.shape
    inner = out_w.shape[2]
    wide = model // shard_rows * pad_rows
    whole = pl.BlockSpec(memory_space=pltpu.VMEM)
    once = lambda shape: pl.BlockSpec((1,) + shape, lambda m: (m,) + (0,) * len(shape))
    out_specs, out_shape = forward_outputs(micro, heads, inner, model, rows, wide)
    return pl.pallas_call(
        functools.partial(attention_forward_kernel, shard_rows=shard_rows, pad_rows=pad_rows),
        grid=(micro,),
        in_specs=[
            pl.BlockSpec((1, 1, lens.shape[2]), lambda m: (m, 0, 0), memory_space=pltpu.SMEM),
            once((model, rows)),
            once((model, rows)),
            whole,
            whole,
            whole,
            whole,
            whole,
        ],
        out_specs=out_specs,
        out_shape=out_shape,
        scratch_shapes=[
            pltpu.VMEM((heads, 2 * (rows // tile) - 1, tile, tile), bf16),
            pltpu.VMEM((model, rows), f32),
        ],
        compiler_params=pltpu.CompilerParams(vmem_limit_bytes=vmem_bytes),
        name="attention_forward",
    )(lens, tok, og, qkv_w, out_w, gains, table, bucket)


class Hidden:
    block = 256
    span = 512

    def __init__(
        self, matrices, normed, normed_t, og, og_t, branch, back, hidden, gate, up, grad_of
    ):
        self.matrices = matrices
        self.normed, self.normed_t, self.og, self.og_t = normed, normed_t, og, og_t
        self.branch, self.back = branch, back
        self.hidden, self.gate, self.up = hidden, gate, up
        self.grad_of = grad_of

    def matrix(self, which, rows=slice(None)):
        return jnp.concatenate([part[rows, :] for part in self.matrices[which]], axis=1)

    def project(self, start, stop):
        def step(b, carry):
            rows = pl.ds(pl.multiple_of(b * self.block, self.block), self.block)
            gate = dot_nn(self.normed[rows, :], self.matrix(0))
            up = dot_nn(self.normed[rows, :], self.matrix(1))
            grad = dot_nn(self.og[rows, :], self.matrix(2))
            cube = gelu_cubic * gate * gate
            t = jnp.tanh(gelu_scale * gate * (1.0 + cube))
            half = 0.5 * (1.0 + t)
            act = gate * half
            slope = half + (0.5 * gelu_scale) * gate * (1.0 - t * t) * (1.0 + 3.0 * cube)
            self.hidden[rows, :] = (act * up).astype(bf16)
            self.gate[rows, :] = (grad * up * slope).astype(bf16)
            self.up[rows, :] = (grad * act).astype(bf16)
            return carry

        lax.fori_loop(start, stop, step, 0)

    def weights(self, start, stop):
        tokens = self.normed.shape[0]
        span = self.span

        def step(b, carry):
            rows = pl.ds(pl.multiple_of(b * span, span), span)
            for which, (left, right) in enumerate(
                (
                    (self.normed_t, self.gate),
                    (self.normed_t, self.up),
                    (self.og_t, self.hidden),
                )
            ):
                grad = dot_nn(left[rows, :], right[...]).astype(bf16)
                for j in range(len(self.matrices[which])):
                    self.grad_of(which, j)[rows, :] = grad[:, j * tile : (j + 1) * tile]
            for which, parts, into in (
                (2, (self.hidden,), self.branch),
                (0, (self.gate, self.up), self.back),
            ):
                for half in range(tokens // span):
                    cols = slice(half * span, (half + 1) * span)
                    total = into[rows, cols]
                    for offset, part in enumerate(parts):
                        total = total + dot_nt(self.matrix(which + offset, rows), part[cols, :])
                    into[rows, cols] = total
            return carry

        lax.fori_loop(start, stop, step, 0)


def feed_forward_kernel(
    normed_hbm,
    normed_t_hbm,
    og_hbm,
    og_t_hbm,
    residual_hbm,
    weight_ref,
    layer_ref,
    back_hbm,
    grad_ref,
    normed_ref,
    normed_t_ref,
    og_ref,
    og_t_ref,
    branch_ref,
    back_ref,
    hidden_ref,
    gate_ref,
    up_ref,
    sems,
    *,
    shard_rows,
    pad_rows,
):
    step = pl.program_id(0)
    col_count = weight_ref.shape[1]
    tokens = normed_ref.shape[0]
    wide = normed_ref.shape[1]
    copies = [
        pltpu.make_async_copy(normed_hbm, normed_ref, sems.at[0]),
        pltpu.make_async_copy(og_hbm, og_ref, sems.at[1]),
        pltpu.make_async_copy(normed_t_hbm, normed_t_ref, sems.at[2]),
        pltpu.make_async_copy(og_t_hbm, og_t_ref, sems.at[3]),
    ]

    @pl.when(step == 0)
    def _():
        fill = pltpu.make_async_copy(residual_hbm, branch_ref, sems.at[5])
        fill.start()
        for copy in copies:
            copy.start()
        for copy in copies:
            copy.wait()
        back_ref[...] = jnp.zeros(back_ref.shape, f32)
        fill.wait()

    matrices = [[weight_ref.at[0, j, which] for j in range(col_count)] for which in range(3)]
    unit = Hidden(
        matrices, normed_ref, normed_t_ref, og_ref, og_t_ref, branch_ref, back_ref, hidden_ref,
        gate_ref, up_ref, lambda which, j: grad_ref.at[0, j, which],
    )
    unit.project(0, tokens // unit.block)
    unit.weights(0, wide // unit.span)

    @pl.when(step == pl.num_programs(0) - 1)
    def _():
        out = pltpu.make_async_copy(back_ref, back_hbm, sems.at[4])
        out.start()
        micro, model, rows = layer_ref.shape
        for m in range(micro):
            for k in range(model // shard_rows):
                source = slice(k * pad_rows, k * pad_rows + shard_rows)
                part = slice(k * shard_rows, (k + 1) * shard_rows)
                layer_ref[m, part, :] = branch_ref[source, m * rows : (m + 1) * rows].astype(bf16)
        out.wait()


def feed_forward(
    normed, normed_t, og, og_t, residual, weights, micro, model, shard_rows, pad_rows
):
    tokens, wide = normed.shape
    rows = tokens // micro
    steps, col_count = weights.shape[:2]
    width = col_count * tile
    anywhere = pl.BlockSpec(memory_space=pl.ANY)
    per_step = lambda: pl.BlockSpec((1,) + weights.shape[1:], lambda t: (t, 0, 0, 0, 0))
    return pl.pallas_call(
        functools.partial(feed_forward_kernel, shard_rows=shard_rows, pad_rows=pad_rows),
        grid=(steps,),
        in_specs=[anywhere] * 5 + [per_step()],
        out_specs=[
            pl.BlockSpec((micro, model, rows), lambda t: (0, 0, 0)),
            anywhere,
            per_step(),
        ],
        out_shape=[
            jax.ShapeDtypeStruct((micro, model, rows), bf16),
            jax.ShapeDtypeStruct((wide, tokens), f32),
            jax.ShapeDtypeStruct(weights.shape, bf16),
        ],
        scratch_shapes=[
            pltpu.VMEM((tokens, wide), bf16),
            pltpu.VMEM((wide, tokens), bf16),
            pltpu.VMEM((tokens, wide), bf16),
            pltpu.VMEM((wide, tokens), bf16),
            pltpu.VMEM((wide, tokens), f32),
            pltpu.VMEM((wide, tokens), f32),
            pltpu.VMEM((tokens, width), bf16),
            pltpu.VMEM((tokens, width), bf16),
            pltpu.VMEM((tokens, width), bf16),
            pltpu.SemaphoreType.DMA((6,)),
        ],
        compiler_params=pltpu.CompilerParams(vmem_limit_bytes=vmem_bytes),
        name="feed_forward",
    )(normed, normed_t, og, og_t, residual, weights)


def lane_fold(values):
    total = values[:, :tile]
    for q in range(1, values.shape[1] // tile):
        total = total + values[:, q * tile : (q + 1) * tile]
    return total


def padded_spans(start, stop, shard_rows, pad_rows):
    spans = []
    while start < stop:
        group, offset = divmod(start, shard_rows)
        size = min(stop - start, shard_rows - offset)
        spans.append((group * pad_rows + offset, size))
        start += size
    return spans


class Padded:
    def __init__(self, ref, shard_rows, pad_rows):
        self.ref, self.shard_rows, self.pad_rows = ref, shard_rows, pad_rows

    def read(self, start, stop):
        spans = padded_spans(start, stop, self.shard_rows, self.pad_rows)
        return jnp.concatenate([self.ref[at : at + size, :] for at, size in spans], axis=0)

    def write(self, start, stop, value):
        done = 0
        for at, size in padded_spans(start, stop, self.shard_rows, self.pad_rows):
            self.ref[at : at + size, :] = value[done : done + size]
            done += size


def attend_back(
    lens_ref,
    tok_ref,
    og_ref,
    wide_ref,
    back_ref,
    qkv_ref,
    attended_ref,
    log_ref,
    qkv_w_ref,
    out_w_ref,
    gains_ref,
    tok_grad_ref,
    tiles_ref,
    diag_ref,
    low_ref,
    grad_qkv_ref,
    fold_ref,
    add_out,
    add_qkv,
    before_heads,
    after_heads,
):
    model, rows = tok_ref.shape[1:]
    inner = attended_ref.shape[1]
    head_count = tiles_ref.shape[0]
    head_dim = inner // head_count
    blocks = rows // tile
    diag_count = 2 * blocks - 1
    size = model // 4
    quarters = [(k * size, (k + 1) * size) for k in range(4)]

    square = jnp.zeros((1, rows), f32)
    cross = jnp.zeros((1, rows), f32)
    for start, stop in quarters:
        x = wide_ref.read(start, stop)
        y = back_ref.read(start, stop)
        square = square + jnp.sum(x * x, axis=0, keepdims=True)
        cross = cross + jnp.sum(x * (y * gains_ref[start:stop, 1:2]), axis=0, keepdims=True)
    scale = lax.rsqrt(square / model + epsilon)
    pull = scale * scale * scale * (cross / model)
    for start, stop in quarters:
        x = wide_ref.read(start, stop)
        y = back_ref.read(start, stop)
        grad = og_ref[0, start:stop, :].astype(f32)
        grad = grad + scale * (y * gains_ref[start:stop, 1:2]) - x * pull
        wide_ref.write(start, stop, grad)
        low_ref[start:stop, :] = grad.astype(bf16)
        fold_ref[1, start:stop, :] += lane_fold(x * scale * y)
    for k, (start, stop) in enumerate(quarters):
        add_out(k, dot_nt(low_ref[start:stop, :], attended_ref[0]))
    grad_attended = dot_tn(out_w_ref[...], low_ref[...]).astype(bf16)
    grad_qkv_ref[0:inner, :] = grad_attended
    before_heads()

    same_doc = doc_labels(lens_ref, 0, rows) == doc_labels(lens_ref, 1, rows)

    def head(h, carry):
        base = pl.multiple_of(h * head_dim, head_dim)
        query_cols = qkv_ref[0, pl.ds(base, head_dim), :]
        key_cols = qkv_ref[0, pl.ds(inner + base, head_dim), :]
        value_cols = qkv_ref[0, pl.ds(2 * inner + base, head_dim), :]
        grad_cols = grad_qkv_ref[pl.ds(base, head_dim), :]
        scores = masked_scores(key_cols.T, query_cols, tiles_ref, h, same_doc, blocks)
        probs = jnp.exp(scores - log_ref[0, h, 0:1, :])
        grad_probs = dot_nn(value_cols.T, grad_cols)
        delta = jnp.sum(probs * grad_probs, axis=0, keepdims=True)
        grad_scores = (probs * (grad_probs - delta)).astype(bf16)
        grad_qkv_ref[pl.ds(2 * inner + base, head_dim), :] = dot_nt(
            grad_cols, probs.astype(bf16)
        ).astype(bf16)
        grad_qkv_ref[pl.ds(base, head_dim), :] = dot_nn(key_cols, grad_scores).astype(bf16)
        grad_qkv_ref[pl.ds(inner + base, head_dim), :] = dot_nt(query_cols, grad_scores).astype(
            bf16
        )
        wide = grad_scores.astype(f32)
        for d in range(diag_count):
            total = None
            for key_block in range(blocks):
                query_block = d - (blocks - 1) + key_block
                if 0 <= query_block < blocks:
                    piece = wide[
                        key_block * tile : (key_block + 1) * tile,
                        query_block * tile : (query_block + 1) * tile,
                    ]
                    total = piece if total is None else total + piece
            diag_ref[h, d] += total
        return carry

    lax.fori_loop(0, head_count, head, 0)
    after_heads()

    square = jnp.zeros((1, rows), f32)
    for start, stop in quarters:
        x = tok_ref[0, start:stop, :].astype(f32)
        square = square + jnp.sum(x * x, axis=0, keepdims=True)
    scale = lax.rsqrt(square / model + epsilon)
    cross = jnp.zeros((1, rows), f32)
    for k, (start, stop) in enumerate(quarters):
        x = tok_ref[0, start:stop, :].astype(f32)
        normed = (x * scale * gains_ref[start:stop, 0:1]).astype(bf16)
        add_qkv(k, dot_nt(normed, grad_qkv_ref[...]))
        y = dot_nn(qkv_w_ref[start:stop, :], grad_qkv_ref[...])
        back_ref.write(start, stop, y)
        cross = cross + jnp.sum(x * (y * gains_ref[start:stop, 0:1]), axis=0, keepdims=True)
        fold_ref[0, start:stop, :] += lane_fold(x * scale * y)
    pull = scale * scale * scale * (cross / model)
    for start, stop in quarters:
        x = tok_ref[0, start:stop, :].astype(f32)
        y = back_ref.read(start, stop)
        grad = wide_ref.read(start, stop) + scale * (y * gains_ref[start:stop, 0:1]) - x * pull
        tok_grad_ref[0, start:stop, :] = grad.astype(bf16)


def dot_exact(a, b, dims):
    return lax.dot_general(
        a, b, ((dims[:1], dims[1:]), ((), ())), preferred_element_type=f32, precision=highest
    )


def bucket_sums(diag_ref, bucket_ref, bucket_count, head_rows):
    head_count, diag_count = diag_ref.shape[:2]
    down = lax.broadcasted_iota(jnp.int32, (tile, tile), 0)
    across = lax.broadcasted_iota(jnp.int32, (tile, tile), 1)
    flip = (down + across == tile - 1).astype(f32)
    onehot = bucket_onehot(bucket_ref, bucket_count).astype(f32)
    rest = jnp.zeros((tile, tile), f32)
    lines = []
    for h in range(head_count):
        carry = jnp.zeros((1, tile), f32)
        pieces = []
        for d in range(diag_count):
            turned = dot_exact(flip, diag_ref[h, d], (1, 0))
            spread = pltpu.roll(
                jnp.concatenate([turned, rest], axis=1), 0, 1, stride=1, stride_axis=0
            )
            sums = jnp.sum(spread, axis=0, keepdims=True)
            pieces.append(sums[:, :tile] + carry)
            carry = sums[:, tile:]
        pieces.append(carry)
        lines.append(jnp.concatenate(pieces, axis=1))
    filler = jnp.zeros((head_rows - head_count, onehot.shape[1]), f32)
    return dot_exact(jnp.concatenate(lines + [filler], axis=0), onehot, (1, 1))


def gain_rows_of(fold_ref, start, stop):
    down = lax.broadcasted_iota(jnp.int32, (16, 2 * tile), 0)
    across = lax.broadcasted_iota(jnp.int32, (16, 2 * tile), 1)
    pick = (across // tile == down).astype(f32)
    both = jnp.concatenate([fold_ref[0, start:stop, :], fold_ref[1, start:stop, :]], axis=1)
    return dot_exact(pick, both, (1, 1))


def attention_backward_kernel(
    lens_ref,
    tok_ref,
    og_ref,
    residual_hbm,
    back_hbm,
    qkv_ref,
    attended_ref,
    log_ref,
    qkv_w_ref,
    out_w_ref,
    gains_ref,
    table_ref,
    bucket_ref,
    tok_grad_ref,
    qkv_grad_ref,
    out_grad_ref,
    table_grad_ref,
    gains_grad_ref,
    wide_ref,
    back_ref,
    tiles_ref,
    diag_ref,
    low_ref,
    grad_qkv_ref,
    fold_ref,
    sems,
    *,
    shard_rows,
    pad_rows,
):
    micro_index = pl.program_id(0)
    model, rows = tok_ref.shape[1:]
    size = model // 4
    start_load(residual_hbm, back_hbm, wide_ref, back_ref, sems, micro_index)

    @pl.when(micro_index == 0)
    def _():
        fill_bias_tiles([table_ref[...]], bucket_ref, tiles_ref)
        diag_ref[...] = jnp.zeros(diag_ref.shape, f32)
        fold_ref[...] = jnp.zeros(fold_ref.shape, f32)
        qkv_grad_ref[...] = jnp.zeros(qkv_grad_ref.shape, f32)
        out_grad_ref[...] = jnp.zeros(out_grad_ref.shape, f32)

    wait_load(residual_hbm, back_hbm, wide_ref, back_ref, sems, micro_index)

    def add_out(k, value):
        out_grad_ref[k * size : (k + 1) * size, :] += value

    def add_qkv(k, value):
        qkv_grad_ref[k * size : (k + 1) * size, :] += value

    nothing = lambda: None
    attend_back(
        lens_ref, tok_ref, og_ref, Padded(wide_ref, shard_rows, pad_rows),
        Padded(back_ref, shard_rows, pad_rows), qkv_ref, attended_ref, log_ref, qkv_w_ref,
        out_w_ref, gains_ref, tok_grad_ref, tiles_ref, diag_ref, low_ref, grad_qkv_ref, fold_ref,
        add_out, add_qkv, nothing, nothing,
    )

    @pl.when(micro_index == pl.num_programs(0) - 1)
    def _():
        gains_grad_ref[...] = gain_rows_of(fold_ref, 0, model)
        head_rows, bucket_count = table_grad_ref.shape
        table_grad_ref[...] = bucket_sums(diag_ref, bucket_ref, bucket_count, head_rows)


def load_copies(residual_hbm, back_hbm, wide_ref, back_ref, sems, m):
    rows = wide_ref.shape[1]
    cols = pl.ds(pl.multiple_of(m * rows, rows), rows)
    return [
        pltpu.make_async_copy(residual_hbm.at[:, cols], wide_ref, sems.at[0]),
        pltpu.make_async_copy(back_hbm.at[:, cols], back_ref, sems.at[1]),
    ]


def start_load(*args):
    for copy in load_copies(*args):
        copy.start()


def wait_load(*args):
    for copy in load_copies(*args):
        copy.wait()


def backward_inputs(lens, heads, inner, model, rows):
    whole = pl.BlockSpec(memory_space=pltpu.VMEM)
    anywhere = pl.BlockSpec(memory_space=pl.ANY)
    once = lambda shape: pl.BlockSpec(
        (1,) + shape, lambda m: (m,) + (0,) * len(shape), pipeline_mode=pl.Buffered(1)
    )
    return [
        pl.BlockSpec((1, 1, lens.shape[2]), lambda m: (m, 0, 0), memory_space=pltpu.SMEM),
        once((model, rows)),
        once((model, rows)),
        anywhere,
        anywhere,
        once((3 * inner, rows)),
        once((inner, rows)),
        once((heads, 8, rows)),
        whole,
        whole,
        whole,
        whole,
        whole,
    ]


def backward_scratch(heads, inner, model, rows, wide):
    diag_count = 2 * (rows // tile) - 1
    return [
        pltpu.VMEM((wide, rows), f32),
        pltpu.VMEM((wide, rows), f32),
        pltpu.VMEM((heads, diag_count, tile, tile), bf16),
        pltpu.VMEM((heads, diag_count, tile, tile), f32),
        pltpu.VMEM((model, rows), bf16),
        pltpu.VMEM((3 * inner, rows), bf16),
        pltpu.VMEM((2, model, tile), f32),
        pltpu.SemaphoreType.DMA((2,)),
    ]


def attention_backward(
    lens, tok, og, residual, back, qkv, attended, log_total, qkv_w, out_w, gains, table, bucket,
    shard_rows, pad_rows,
):
    micro, model, rows = tok.shape
    inner = out_w.shape[1]
    heads = log_total.shape[1]
    wide = back.shape[0]
    whole = pl.BlockSpec(memory_space=pltpu.VMEM)
    return pl.pallas_call(
        functools.partial(attention_backward_kernel, shard_rows=shard_rows, pad_rows=pad_rows),
        grid=(micro,),
        in_specs=backward_inputs(lens, heads, inner, model, rows),
        out_specs=[pl.BlockSpec((1, model, rows), lambda m: (m, 0, 0))] + [whole] * 4,
        out_shape=[
            jax.ShapeDtypeStruct((micro, model, rows), bf16),
            jax.ShapeDtypeStruct((model, 3 * inner), f32),
            jax.ShapeDtypeStruct((model, inner), f32),
            jax.ShapeDtypeStruct((table.shape[0], table.shape[1]), f32),
            jax.ShapeDtypeStruct((16, model), f32),
        ],
        scratch_shapes=backward_scratch(heads, inner, model, rows, wide),
        compiler_params=pltpu.CompilerParams(vmem_limit_bytes=vmem_bytes),
        name="attention_backward",
    )(lens, tok, og, residual, back, qkv, attended, log_total, qkv_w, out_w, gains, table, bucket)


class Place:
    def __init__(self, row_count):
        self.row_count = row_count
        self.y = lax.axis_index("dp")
        self.z = lax.axis_index("row")
        col = lax.axis_index("col")
        self.x = col // 2
        self.core = col % 2
        self.near_x = self.x + (1 - self.core) * (1 - 2 * self.x)
        self.near_y = self.y + self.core * (1 - 2 * self.y)
        self.far_x = self.x + self.core * (1 - 2 * self.x)
        self.far_y = self.y + (1 - self.core) * (1 - 2 * self.y)

    def at(self, x, y, z, core):
        return (y, z, 2 * x + core)

    def near(self):
        return self.at(self.near_x, self.near_y, self.z, self.core)

    def far(self):
        return self.at(self.far_x, self.far_y, self.z, self.core)

    def partner(self):
        return self.at(self.x, self.y, self.z, 1 - self.core)

    def beside_y(self):
        return self.at(self.x, 1 - self.y, self.z, self.core)

    def beside_x(self):
        return self.at(1 - self.x, self.y, self.z, self.core)

    def along(self, step):
        return self.at(self.x, self.y, lax.rem(self.z + step, self.row_count), self.core)

    def greet(self, across=False):
        barrier = pltpu.get_barrier_semaphore()
        others = [self.near(), self.far(), self.partner()]
        for step in range(1, self.row_count):
            others.append(self.along(step))
            if across:
                z = lax.rem(self.z + step, self.row_count)
                others.append(self.at(1 - self.x, self.y, z, self.core))
        for other in others:
            pl.semaphore_signal(barrier, inc=1, device_id=other, device_id_type=MESH)
        pl.semaphore_wait(barrier, len(others))


def send(source, target, send_sem, recv_sem, device):
    return pltpu.make_async_remote_copy(
        src_ref=source,
        dst_ref=target,
        send_sem=send_sem,
        recv_sem=recv_sem,
        device_id=device,
        device_id_type=MESH,
    )


def gather_semaphores(steps, row_count):
    dma = pltpu.SemaphoreType.DMA
    return [
        dma((steps,)),
        dma((2, steps, row_count - 1)),
        dma((2, steps, 3)),
        dma((2, steps, 4)),
    ]


class Gather:
    def __init__(self, place, shard_ref, full_ref, sems, base=0):
        self.place, self.shard, self.full, self.base = place, shard_ref, full_ref, base
        self.local, self.line, self.cross, self.pair = sems
        self.pad_rows = shard_ref.shape[2]
        self.unit_rows = self.pad_rows * place.row_count

    def unit(self, t, x, y, core):
        rows = pl.ds(pl.multiple_of(y * self.unit_rows, self.unit_rows), self.unit_rows)
        return self.full.at[t - self.base, 2 * x + core, :, rows, :]

    def own(self, t):
        p = self.place
        index = p.y * p.row_count + p.z
        rows = pl.ds(pl.multiple_of(index * self.pad_rows, self.pad_rows), self.pad_rows)
        return self.full.at[t - self.base, 2 * p.x + p.core, :, rows, :]

    def copy_local(self, t):
        return pltpu.make_async_copy(self.shard.at[t], self.own(t), self.local.at[t])

    def copy_line(self, t, step):
        return send(
            self.shard.at[t],
            self.own(t),
            self.line.at[0, t, step - 1],
            self.line.at[1, t, step - 1],
            self.place.along(step),
        )

    def copy_cross(self, t, which):
        p = self.place
        x, y = ((p.x, p.y), (p.x, p.y), (p.near_x, p.near_y))[which]
        unit = self.unit(t, x, y, p.core)
        device = p.near() if which == 0 else p.far()
        return send(unit, unit, self.cross.at[0, t, which], self.cross.at[1, t, which], device)

    def copy_pair(self, t, which):
        p = self.place
        x, y = (
            (p.x, p.y),
            (p.near_x, p.near_y),
            (p.far_x, p.far_y),
            (1 - p.x, 1 - p.y),
        )[which]
        unit = self.unit(t, x, y, p.core)
        return send(
            unit, unit, self.pair.at[0, t, which], self.pair.at[1, t, which], p.partner()
        )

    def begin(self, t):
        self.copy_local(t).start()
        for step in range(1, self.place.row_count):
            self.copy_line(t, step).start()

    def spread(self, t):
        self.copy_local(t).wait()
        for step in range(1, self.place.row_count):
            self.copy_line(t, step).wait_recv()
        self.copy_cross(t, 0).start()
        self.copy_cross(t, 1).start()
        self.copy_pair(t, 0).start()

    def relay(self, t):
        self.copy_cross(t, 0).wait_recv()
        self.copy_cross(t, 2).start()
        self.copy_pair(t, 1).start()
        self.copy_cross(t, 1).wait_recv()
        self.copy_pair(t, 2).start()

    def settle(self, t):
        self.copy_cross(t, 2).wait_recv()
        self.copy_pair(t, 3).start()

    def finish(self, t):
        for which in range(4):
            self.copy_pair(t, which).wait_recv()

    def drain(self, t):
        for step in range(1, self.place.row_count):
            self.copy_line(t, step).wait_send()
        for which in range(3):
            self.copy_cross(t, which).wait_send()
        for which in range(4):
            self.copy_pair(t, which).wait_send()


class Share:
    def __init__(self, place, pairs, sems):
        self.place, self.pairs, self.sems = place, pairs, sems

    def rows(self, ref, core):
        half = ref.shape[0] // 2
        return pl.ds(pl.multiple_of(core * half, half), half)

    def copy_local(self, i):
        own, full = self.pairs[i]
        return pltpu.make_async_copy(own, full.at[self.place.y], self.sems.at[0, i, 0])

    def copy_over(self, i):
        own, full = self.pairs[i]
        p = self.place
        rows = self.rows(own, p.core)
        return send(
            own.at[rows, :],
            full.at[p.y, rows, :],
            self.sems.at[0, i, 1],
            self.sems.at[1, i, 1],
            p.beside_y(),
        )

    def copy_pair(self, i):
        own, full = self.pairs[i]
        p = self.place
        part = full.at[1 - p.y, self.rows(own, p.core), :]
        return send(part, part, self.sems.at[0, i, 2], self.sems.at[1, i, 2], p.partner())

    def begin(self):
        for i in range(len(self.pairs)):
            self.copy_over(i).start()
        for i in range(len(self.pairs)):
            self.copy_local(i).start()

    def relay(self):
        for i in range(len(self.pairs)):
            self.copy_over(i).wait_recv()
            self.copy_pair(i).start()

    def finish(self):
        for i in range(len(self.pairs)):
            self.copy_local(i).wait()
            self.copy_pair(i).wait_recv()

    def drain(self):
        for i in range(len(self.pairs)):
            self.copy_over(i).wait_send()
            self.copy_pair(i).wait_send()


def add_into(into, other):
    into[...] = into[...] + other[...]


def tables_of(small_ref, table_rows, bucket_part):
    return [small_ref[y, 16 : 16 + table_rows, 0:bucket_part] for y in range(2)]


def fused_forward_kernel(
    lens_ref, tok_ref, og_ref, bucket_ref, shard_ref, qkv_own, out_own, small_own,
    normed_ref, normed_t_ref, og_pad_ref, og_pad_t_ref, qkv_ref, attended_ref, log_ref,
    residual_ref, full_ref, qkv_full, out_full, small_full, gains_full,
    tiles_ref, scaled_ref, gains_ref, qkv_w_ref, out_w_ref, small_ref,
    local, line, cross, pair, share_sems, keep_sems,
    *, row_count, shard_rows, pad_rows, table_rows, bucket_part,
):
    micro_index = pl.program_id(0)
    early = full_ref.shape[0]
    part = qkv_own.shape[0]
    place = Place(row_count)
    gather = Gather(place, shard_ref, full_ref, (local, line, cross, pair))
    share = Share(
        place,
        [(small_own, small_ref), (qkv_own, qkv_w_ref), (out_own, out_w_ref)],
        share_sems,
    )
    keeps = [
        pltpu.make_async_copy(source, target, keep_sems.at[i])
        for i, (source, target) in enumerate(
            (
                (qkv_w_ref, qkv_full),
                (out_w_ref, out_full),
                (small_ref, small_full),
                (gains_ref, gains_full),
            )
        )
    ]

    @pl.when(micro_index == 0)
    def _():
        place.greet()
        share.begin()
        for t in range(early):
            gather.begin(t)

    pad_cotangent(og_ref, og_pad_ref, og_pad_t_ref, shard_rows, pad_rows)

    @pl.when(micro_index == 0)
    def _():
        gather.spread(0)
        share.relay()
        for t in range(1, early):
            gather.spread(t)
        share.finish()
        for y in range(2):
            turned = small_ref[y, 0:16, :].astype(f32).T
            gains_ref[y * part : (y + 1) * part, :] = turned[:part, :]
        for keep in keeps:
            keep.start()
        fill_bias_tiles(tables_of(small_ref, table_rows, bucket_part), bucket_ref, tiles_ref)

    def between():
        @pl.when(micro_index == 0)
        def _():
            gather.relay(0)

        @pl.when(micro_index == 1)
        def _():
            gather.settle(0)

    attend(
        lens_ref, tok_ref, qkv_w_ref, out_w_ref, gains_ref, normed_ref, normed_t_ref, qkv_ref,
        attended_ref, log_ref, residual_ref, tiles_ref, scaled_ref, shard_rows, pad_rows, between,
    )

    @pl.when(micro_index == 0)
    def _():
        for t in range(1, early):
            gather.relay(t)

    @pl.when(micro_index == 1)
    def _():
        for t in range(1, early):
            gather.settle(t)
        share.drain()
        for keep in keeps:
            keep.wait()
        for t in range(early):
            gather.finish(t)
            gather.drain(t)


def fused_forward(
    lens, tok, og, bucket, shard, qkv_w, out_w, small, heads, early, shard_rows, pad_rows,
    row_count, col_count, bucket_part,
):
    micro, model, rows = tok.shape
    inner = out_w.shape[1]
    steps, kinds = shard.shape[:2]
    wide = model // shard_rows * pad_rows
    anywhere = pl.BlockSpec(memory_space=pl.ANY)
    whole = pl.BlockSpec(memory_space=pltpu.VMEM)
    once = lambda shape: pl.BlockSpec((1,) + shape, lambda m: (m,) + (0,) * len(shape))
    double = lambda a: jax.ShapeDtypeStruct((2,) + a.shape, a.dtype)
    out_specs, out_shape = forward_outputs(micro, heads, inner, model, rows, wide)
    dma = pltpu.SemaphoreType.DMA
    return pl.pallas_call(
        functools.partial(
            fused_forward_kernel, row_count=row_count, shard_rows=shard_rows, pad_rows=pad_rows,
            table_rows=16, bucket_part=bucket_part,
        ),
        grid=(micro,),
        in_specs=[
            pl.BlockSpec((1, 1, lens.shape[2]), lambda m: (m, 0, 0), memory_space=pltpu.SMEM),
            once((model, rows)),
            once((model, rows)),
            whole,
        ]
        + [anywhere] * 4,
        out_specs=out_specs + [anywhere] * 5,
        out_shape=out_shape
        + [
            jax.ShapeDtypeStruct((early, col_count, kinds, wide, tile), bf16),
            double(qkv_w),
            double(out_w),
            double(small),
            jax.ShapeDtypeStruct((model, 16), f32),
        ],
        scratch_shapes=[
            pltpu.VMEM((heads, 2 * (rows // tile) - 1, tile, tile), bf16),
            pltpu.VMEM((model, rows), f32),
            pltpu.VMEM((model, 16), f32),
            pltpu.VMEM((2,) + qkv_w.shape, bf16),
            pltpu.VMEM((2,) + out_w.shape, bf16),
            pltpu.VMEM((2,) + small.shape, bf16),
        ]
        + gather_semaphores(steps, row_count)
        + [dma((2, 3, 3)), dma((4,))],
        compiler_params=pltpu.CompilerParams(
            collective_id=0, has_side_effects=True, vmem_limit_bytes=vmem_bytes
        ),
        name="fused_forward",
    )(lens, tok, og, bucket, shard, qkv_w, out_w, small)


def fused_hidden_kernel(
    normed_hbm, normed_t_hbm, og_hbm, og_t_hbm, residual_hbm, first_ref, shard_ref,
    layer_hbm, back_hbm, sums_hbm, rest_ref, landed_hbm,
    normed_ref, normed_t_ref, og_ref, og_t_ref, branch_ref, back_ref, hidden_ref, gate_ref, up_ref,
    weight_ref, grad_ref, other_ref, layer_ref,
    local, line, cross, pair, load_sems, weight_sems, store_sems, swap_sems, far_sems,
    credit,
    *, row_count, shard_rows, pad_rows,
):
    t = pl.program_id(0)
    steps, col_count = shard_ref.shape[0], weight_ref.shape[1]
    early = first_ref.shape[0]
    tokens, wide = normed_ref.shape
    place = Place(row_count)
    slot = lax.rem(t, 2)
    gather = Gather(place, shard_ref, rest_ref, (local, line, cross, pair), early)
    reduce = Reduce(place, sums_hbm, landed_hbm, far_sems)
    ahead = landed_hbm.shape[0]

    def load_early(q):
        s = lax.rem(q, 2)
        return pltpu.make_async_copy(first_ref.at[q], weight_ref.at[s], weight_sems.at[s])

    def load_late(q):
        s = lax.rem(q, 2)
        return pltpu.make_async_copy(rest_ref.at[q - early], weight_ref.at[s], weight_sems.at[s])

    def swap(q):
        s = lax.rem(q, 2)
        return send(
            grad_ref.at[s, :, 1 - place.core], other_ref.at[s], swap_sems.at[0, q],
            swap_sems.at[1, q], place.partner(),
        )

    def store(q):
        s = lax.rem(q, 2)
        return pltpu.make_async_copy(
            grad_ref.at[s, :, place.core], sums_hbm.at[q], store_sems.at[s]
        )

    def fold(q):
        s = lax.rem(q, 2)
        swap(q).wait_recv()
        for x in range(col_count // 2):
            for kind in range(3):
                add_into(grad_ref.at[s, x, place.core, kind], other_ref.at[s, x, kind])
        store(q).start()

        @pl.when(q < steps - 2)
        def _():
            pl.semaphore_signal(credit, 1, device_id=place.partner(), device_id_type=MESH)

    def late(q):
        return (q >= early) & (q < steps)

    @pl.when(t == 0)
    def _():
        loads = [
            pltpu.make_async_copy(source, target, load_sems.at[i])
            for i, (source, target) in enumerate(
                (
                    (normed_hbm, normed_ref),
                    (og_hbm, og_ref),
                    (normed_t_hbm, normed_t_ref),
                    (og_t_hbm, og_t_ref),
                    (residual_hbm, branch_ref),
                )
            )
        ]
        load_early(0).start()
        for load in loads:
            load.start()
        place.greet()
        for q in range(early, steps):
            gather.begin(q)
        back_ref[...] = jnp.zeros(back_ref.shape, f32)
        for load in loads:
            load.wait()
        for q in range(early, 4):
            gather.spread(q)

    @pl.when(t < early)
    def _():
        load_early(t).wait()

    @pl.when(t >= early)
    def _():
        load_late(t).wait()

    weights_now = weight_ref.at[slot]
    matrices = [[weights_now.at[j, which] for j in range(col_count)] for which in range(3)]
    unit = Hidden(
        matrices, normed_ref, normed_t_ref, og_ref, og_t_ref, branch_ref, back_ref, hidden_ref,
        gate_ref, up_ref, lambda which, j: grad_ref.at[slot, j // 2, j % 2, which],
    )
    unit.project(0, tokens // unit.block)

    @pl.when(t >= 1)
    def _():
        fold(t - 1)

    @pl.when(t >= 2)
    def _():
        swap(t - 2).wait_send()
        store(t - 2).wait()

    def send_far(step, chunks):
        @pl.when(t == step)
        def _():
            for q in chunks:
                reduce.begin(q)

    send_far(steps - 2, [2])

    spans = wide // unit.span
    unit.weights(0, spans - 1)

    @pl.when(late(t + 2))
    def _():
        gather.relay(t + 2)

    @pl.when(late(t + 4))
    def _():
        gather.spread(t + 4)

    @pl.when(late(t + 1))
    def _():
        gather.settle(t + 1)

    @pl.when(t + 1 < early)
    def _():
        load_early(t + 1).start()

    send_far(steps - 3, [0, 1])
    send_far(steps - 2, [3])

    unit.weights(spans - 1, spans)

    @pl.when(late(t + 1))
    def _():
        gather.finish(t + 1)
        load_late(t + 1).start()

    @pl.when(t >= 2)
    def _():
        pl.semaphore_wait(credit, 1)

    swap(t).start()

    @pl.when(t == steps - 1)
    def _():
        out = pltpu.make_async_copy(back_ref, back_hbm, load_sems.at[0])
        out.start()
        rows = layer_ref.shape[1]
        for m in range(tokens // rows):
            for k in range(wide // pad_rows):
                source = slice(k * pad_rows, k * pad_rows + shard_rows)
                part = slice(k * shard_rows, (k + 1) * shard_rows)
                layer_ref[part, :] = branch_ref[source, m * rows : (m + 1) * rows].astype(bf16)
            layer_out = pltpu.make_async_copy(layer_ref, layer_hbm.at[m], load_sems.at[1])
            layer_out.start()
            layer_out.wait()
        fold(t)
        swap(t - 1).wait_send()
        swap(t).wait_send()
        store(t - 1).wait()
        store(t).wait()
        out.wait()
        for q in range(early, steps):
            gather.drain(q)
        for q in range(ahead):
            for which in range(2):
                reduce.copy_far(q, which).wait()


def fused_hidden(
    normed, normed_t, og, og_t, residual, first, shard, micro, model, shard_rows, pad_rows,
    row_count, ahead,
):
    tokens, wide = normed.shape
    rows = tokens // micro
    steps, kinds = shard.shape[:2]
    early, col_count = first.shape[:2]
    x_count = col_count // 2
    width = col_count * tile
    anywhere = pl.BlockSpec(memory_space=pl.ANY)
    dma = pltpu.SemaphoreType.DMA
    return pl.pallas_call(
        functools.partial(
            fused_hidden_kernel, row_count=row_count, shard_rows=shard_rows, pad_rows=pad_rows
        ),
        grid=(steps,),
        in_specs=[anywhere] * 7,
        out_specs=[anywhere] * 5,
        out_shape=[
            jax.ShapeDtypeStruct((micro, model, rows), bf16),
            jax.ShapeDtypeStruct((wide, tokens), f32),
            jax.ShapeDtypeStruct((steps, x_count, kinds, wide, tile), bf16),
            jax.ShapeDtypeStruct((steps - early,) + first.shape[1:], bf16),
            jax.ShapeDtypeStruct((ahead, 2, kinds, pad_rows * row_count, tile), bf16),
        ],
        scratch_shapes=[
            pltpu.VMEM((tokens, wide), bf16),
            pltpu.VMEM((wide, tokens), bf16),
            pltpu.VMEM((tokens, wide), bf16),
            pltpu.VMEM((wide, tokens), bf16),
            pltpu.VMEM((wide, tokens), f32),
            pltpu.VMEM((wide, tokens), f32),
            pltpu.VMEM((tokens, width), bf16),
            pltpu.VMEM((tokens, width), bf16),
            pltpu.VMEM((tokens, width), bf16),
            pltpu.VMEM((2, col_count, kinds, wide, tile), bf16),
            pltpu.VMEM((2, x_count, 2, kinds, wide, tile), bf16),
            pltpu.VMEM((2, x_count, kinds, wide, tile), bf16),
            pltpu.VMEM((model, rows), bf16),
        ]
        + gather_semaphores(steps, row_count)
        + [
            dma((5,)),
            dma((2,)),
            dma((2,)),
            dma((2, steps)),
            dma((2, ahead, 2)),
            pltpu.SemaphoreType.REGULAR,
        ],
        compiler_params=pltpu.CompilerParams(
            collective_id=1, has_side_effects=True, vmem_limit_bytes=vmem_bytes
        ),
        name="fused_hidden",
    )(normed, normed_t, og, og_t, residual, first, shard)


class Reduce:
    slots = 2

    def __init__(
        self, place, source, second, cross, landed=None, landed_sems=None, stage=None, third=None,
        fourth=None, load=None, line=None,
    ):
        self.place, self.source, self.second, self.cross = place, source, second, cross
        self.landed, self.landed_sems, self.stage = landed, landed_sems, stage
        self.third, self.fourth, self.load, self.line = third, fourth, load, line
        self.unit_rows = second.shape[3]
        self.pad_rows = self.unit_rows // place.row_count
        self.ahead = 0 if landed is None else landed.shape[0]

    def unit(self, t, x, y):
        rows = pl.ds(pl.multiple_of(y * self.unit_rows, self.unit_rows), self.unit_rows)
        return self.source.at[t, x, :, rows, :]

    def shard(self, row):
        return pl.ds(pl.multiple_of(row * self.pad_rows, self.pad_rows), self.pad_rows)

    def copy_own(self, t, which):
        p = self.place
        slot = t % self.slots
        x, y = ((p.x, p.y), (p.near_x, p.near_y))[which]
        return pltpu.make_async_copy(
            self.unit(t, x, y), self.stage.at[slot, which], self.load.at[slot, which]
        )

    def copy_far(self, t, which):
        p = self.place
        x, y = ((p.far_x, p.far_y), (1 - p.x, 1 - p.y))[which]
        return send(
            self.unit(t, x, y), self.second.at[t, which], self.cross.at[0, t, which],
            self.cross.at[1, t, which], p.far(),
        )

    def copy_near(self, t):
        return send(
            self.second.at[t, 1], self.third.at[t], self.cross.at[0, t, 2],
            self.cross.at[1, t, 2], self.place.near(),
        )

    def copy_line(self, t, i):
        p = self.place
        beside = p.z + 1 - 2 * lax.rem(p.z, 2)
        shard = (beside, lax.rem(beside + 2, 4), lax.rem(p.z + 2, 4))[i]
        to = beside if i < 2 else shard
        return send(
            self.second.at[t, 0, :, self.shard(shard), :], self.fourth.at[t, i],
            self.line.at[0, t, i], self.line.at[1, t, i], p.at(p.x, p.y, to, p.core),
        )

    def copy_landed(self, t):
        return pltpu.make_async_copy(
            self.landed.at[t], self.second.at[t], self.landed_sems.at[t]
        )

    def load_own(self, t):
        for which in range(2):
            self.copy_own(t, which).start()

    def begin(self, t):
        self.copy_far(t, 1).start()
        self.copy_far(t, 0).start()

    def fold_far(self, t):
        self.copy_own(t, 1).wait()
        if t < self.ahead:
            self.copy_landed(t).wait()
        else:
            self.copy_far(t, 1).wait_recv()
        slot = t % self.slots
        for kind in range(3):
            add_into(self.second.at[t, 1, kind], self.stage.at[slot, 1, kind])
        self.copy_near(t).start()
        self.copy_own(t, 0).wait()
        if t >= self.ahead:
            self.copy_far(t, 0).wait_recv()
        for kind in range(3):
            add_into(self.second.at[t, 0, kind], self.stage.at[slot, 0, kind])

    def fold_near(self, t):
        self.copy_near(t).wait_recv()
        for kind in range(3):
            add_into(self.second.at[t, 0, kind], self.third.at[t, kind])
        self.copy_line(t, 0).start()
        self.copy_line(t, 1).start()

    def fold_line(self, t):
        p = self.place
        for i in range(2):
            self.copy_line(t, i).wait_recv()
        for i, shard in ((1, lax.rem(p.z + 2, 4)), (0, p.z)):
            for kind in range(3):
                add_into(
                    self.second.at[t, 0, kind, self.shard(shard), :], self.fourth.at[t, i, kind]
                )
            if i == 1:
                self.copy_line(t, 2).start()

    def total(self, t, kind):
        own = self.second[t, 0, kind, self.shard(self.place.z), :].astype(f32)
        return own + self.fourth[t, 2, kind].astype(f32)

    def wait_line(self, t):
        self.copy_line(t, 2).wait_recv()

    def drain(self, t):
        if t >= self.ahead:
            for which in range(2):
                self.copy_far(t, which).wait_send()
        self.copy_near(t).wait_send()
        for i in range(3):
            self.copy_line(t, i).wait_send()


class Dense:
    def __init__(self, place, source, first, second, third, fourth, piece, out, sems):
        self.place, self.source = place, source
        self.first, self.second, self.third, self.fourth = first, second, third, fourth
        self.piece, self.out, self.sems = piece, out, sems
        self.half, self.quarter, self.piece_rows = (
            second.shape[0], third.shape[0], piece.shape[0],
        )
        self.others = range(1, place.row_count)

    def rows(self, start, size):
        return pl.ds(pl.multiple_of(start, 16), size)

    def sem(self, i):
        return self.sems.at[0, i], self.sems.at[1, i]

    def half_rows(self, core):
        return self.rows(core * self.half, self.half)

    def quarter_rows(self, x):
        return self.rows(self.place.core * self.half + x * self.quarter, self.quarter)

    def piece_at(self, step):
        p = self.place
        z = lax.rem(p.z + step, p.row_count)
        start = p.core * self.half + p.x * self.quarter + z * self.piece_rows
        return self.rows(start, self.piece_rows)

    def copy_pair(self):
        p = self.place
        return send(
            self.source.at[:, self.half_rows(1 - p.core), :], self.first, *self.sem(0), p.partner()
        )

    def copy_y(self):
        p = self.place
        part = self.source.at[1 - p.y, self.half_rows(p.core), :]
        return send(part, self.second, *self.sem(1), p.beside_y())

    def copy_x(self):
        p = self.place
        part = self.source.at[p.y, self.quarter_rows(1 - p.x), :]
        return send(part, self.third, *self.sem(2), p.beside_x())

    def copy_piece(self, step):
        part = self.source.at[self.place.y, self.piece_at(step), :]
        return send(part, self.fourth.at[step - 1], *self.sem(5 + step), self.place.along(step))

    def keep_piece(self):
        return pltpu.make_async_copy(
            self.piece, self.out.at[self.piece_at(0), :], self.sems.at[0, 3]
        )

    def back_piece(self, step):
        index = 5 + self.place.row_count + step
        part = self.out.at[self.piece_at(0), :]
        return send(self.piece, part, *self.sem(index), self.place.along(step))

    def back_x(self):
        part = self.out.at[self.quarter_rows(self.place.x), :]
        return send(part, part, *self.sem(4), self.place.beside_x())

    def back_pair(self):
        part = self.out.at[self.half_rows(self.place.core), :]
        return send(part, part, *self.sem(5), self.place.partner())

    def begin(self):
        self.copy_pair().start()

    def fold_pair(self):
        p = self.place
        self.copy_pair().wait_recv()
        rows = self.half_rows(p.core)
        add_into(self.source.at[1 - p.y, rows, :], self.first.at[1 - p.y])
        self.copy_y().start()
        add_into(self.source.at[p.y, rows, :], self.first.at[p.y])

    def fold_y(self):
        p = self.place
        self.copy_y().wait_recv()
        add_into(self.source.at[p.y, self.half_rows(p.core), :], self.second)
        self.copy_x().start()

    def fold_x(self):
        p = self.place
        self.copy_x().wait_recv()
        add_into(self.source.at[p.y, self.quarter_rows(p.x), :], self.third)
        for step in self.others:
            self.copy_piece(step).start()

    def fold_pieces(self):
        for step in self.others:
            self.copy_piece(step).wait_recv()
        total = self.source[self.place.y, self.piece_at(0), :].astype(f32)
        for step in self.others:
            total = total + self.fourth[step - 1].astype(f32)
        self.piece[...] = total.astype(bf16)
        self.keep_piece().start()
        for step in self.others:
            self.back_piece(step).start()

    def return_x(self):
        self.keep_piece().wait()
        for step in self.others:
            self.back_piece(step).wait_recv()
        self.back_x().start()

    def return_pair(self):
        self.back_x().wait_recv()
        self.back_pair().start()

    def finish(self):
        self.back_pair().wait_recv()
        for copy in (
            self.copy_pair(), self.copy_y(), self.copy_x(), self.back_x(), self.back_pair(),
        ):
            copy.wait_send()
        for step in self.others:
            self.copy_piece(step).wait_send()
            self.back_piece(step).wait_send()


def dense_lanes(inner):
    tiles = 3 * inner // tile
    cut = (tiles + 1) // 2 * tile
    return [(3 * inner, inner), (0, cut), (cut, 3 * inner - cut)]


def fused_backward_kernel(
    lens_ref, tok_ref, og_ref, residual_hbm, back_hbm, qkv_ref, attended_ref, log_ref, qkv_w_ref,
    out_w_ref, gains_ref, small_ref, bucket_ref, source_ref, landed_ref,
    tok_grad_ref, inner_ref, outer_ref, dense_out,
    wide_ref, back_ref, tiles_ref, diag_ref, low_ref, grad_qkv_ref, fold_ref, load_sems,
    stage, second, third, fourth,
    dense_ref, load, cross, line, landed_sems, *dense_scratch, row_count, shard_rows, pad_rows, bucket_part,
):
    micro_index = pl.program_id(0)
    model, rows = tok_ref.shape[1:]
    inner = attended_ref.shape[1]
    part = model // 2
    quarter = model // 4
    steps = source_ref.shape[0]
    place = Place(row_count)
    reduce = Reduce(
        place, source_ref, second, cross, landed_ref, landed_sems, stage, third, fourth, load, line
    )
    streams = []
    for i, (start, size) in enumerate(dense_lanes(inner)):
        first, swapped, across, pieces, piece, sems = dense_scratch[6 * i : 6 * i + 6]
        lanes = pl.ds(start, size)
        streams.append(
            Dense(
                place, dense_ref.at[:, :, lanes], first, swapped, across, pieces, piece,
                dense_out.at[:, lanes], sems,
            )
        )
    out, left, right = streams

    def finish_chunk(t):
        reduce.wait_line(t)
        lanes = slice(t * tile, (t + 1) * tile)
        for kind in range(2):
            inner_ref[kind, :, lanes] = reduce.total(t, kind)[:shard_rows]
        outer_ref[:, lanes] = reduce.total(t, 2)[:shard_rows]

    def group(n):
        if n < steps:
            reduce.fold_far(n)
            if n + reduce.slots < steps:
                reduce.load_own(n + reduce.slots)
        if 0 <= n - 1 < steps:
            reduce.fold_near(n - 1)
        if 0 <= n - 2 < steps:
            reduce.fold_line(n - 2)
        if 0 <= n - 3 < steps:
            finish_chunk(n - 3)

    start_load(residual_hbm, back_hbm, wide_ref, back_ref, load_sems, micro_index)

    @pl.when(micro_index == 0)
    def _():
        for t in range(reduce.slots):
            reduce.load_own(t)
        for t in range(reduce.ahead):
            reduce.copy_landed(t).start()
        place.greet()
        group(0)
        fill_bias_tiles(tables_of(small_ref, 16, bucket_part), bucket_ref, tiles_ref)
        diag_ref[...] = jnp.zeros(diag_ref.shape, f32)
        fold_ref[...] = jnp.zeros(fold_ref.shape, f32)
        dense_ref[...] = jnp.zeros(dense_ref.shape, bf16)

    wait_load(residual_hbm, back_hbm, wide_ref, back_ref, load_sems, micro_index)

    def add(k, start, value):
        at = (k // 2, slice((k % 2) * quarter, (k % 2 + 1) * quarter), slice(start, start + value.shape[1]))
        dense_ref[at] = (dense_ref[at].astype(f32) + value).astype(bf16)

    def before_heads():
        @pl.when(micro_index == 0)
        def _():
            group(1)
            for t in range(reduce.ahead, steps):
                reduce.begin(t)

        @pl.when(micro_index == 1)
        def _():
            out.begin()
            group(3)

    def after_heads():
        @pl.when(micro_index == 0)
        def _():
            group(2)

        @pl.when(micro_index == 1)
        def _():
            out.fold_pair()
            group(4)

    attend_back(
        lens_ref, tok_ref, og_ref, Padded(wide_ref, shard_rows, pad_rows),
        Padded(back_ref, shard_rows, pad_rows), qkv_ref, attended_ref, log_ref, qkv_w_ref,
        out_w_ref, gains_ref, tok_grad_ref, tiles_ref, diag_ref, low_ref, grad_qkv_ref, fold_ref,
        lambda k, value: add(k, 3 * inner, value), lambda k, value: add(k, 0, value),
        before_heads, after_heads,
    )

    @pl.when(micro_index == 1)
    def _():
        half = bucket_part
        sums = bucket_sums(diag_ref, bucket_ref, 2 * half, 16).astype(bf16)
        for y in range(2):
            gains = gain_rows_of(fold_ref, y * part, (y + 1) * part)
            dense_ref[y, part : part + 16, 0:part] = gains.astype(bf16)
            dense_ref[y, part + 16 : part + 32, 0:half] = sums[:, y * half : (y + 1) * half]
        left.begin()
        right.begin()
        out.fold_y()
        group(5)
        left.fold_pair()
        right.fold_pair()
        out.fold_x()
        group(6)
        left.fold_y()
        right.fold_y()
        out.fold_pieces()
        group(7)
        left.fold_x()
        right.fold_x()
        out.return_x()
        group(8)
        left.fold_pieces()
        right.fold_pieces()
        out.return_pair()
        for n in range(9, steps + 3):
            group(n)
        left.return_x()
        right.return_x()
        left.return_pair()
        right.return_pair()
        for stream in streams:
            stream.finish()
        for t in range(steps):
            reduce.drain(t)


def fused_backward(
    lens, tok, og, residual, back, qkv, attended, log_total, qkv_w, out_w, gains, small, bucket,
    source, landed, dense_rows, shard_rows, pad_rows, row_count, bucket_part,
):
    micro, model, rows = tok.shape
    inner = out_w.shape[1]
    heads = log_total.shape[1]
    steps, x_count, kinds, wide, _ = source.shape
    unit_rows = pad_rows * row_count
    slots = Reduce.slots
    width = 4 * inner
    half = dense_rows // 2
    piece_rows = half // (2 * row_count)
    hidden = steps * tile
    anywhere = pl.BlockSpec(memory_space=pl.ANY)
    inside = pl.BlockSpec(memory_space=pltpu.VMEM)
    dma = pltpu.SemaphoreType.DMA
    dense_buffers = []
    for _, size in dense_lanes(inner):
        dense_buffers += [
            pltpu.VMEM((2, half, size), bf16),
            pltpu.VMEM((half, size), bf16),
            pltpu.VMEM((half // 2, size), bf16),
            pltpu.VMEM((row_count - 1, piece_rows, size), bf16),
            pltpu.VMEM((piece_rows, size), bf16),
            dma((2, 6 + 2 * row_count)),
        ]
    return pl.pallas_call(
        functools.partial(
            fused_backward_kernel, row_count=row_count, shard_rows=shard_rows, pad_rows=pad_rows,
            bucket_part=bucket_part,
        ),
        grid=(micro,),
        in_specs=backward_inputs(lens, heads, inner, model, rows) + [anywhere] * 2,
        out_specs=[
            pl.BlockSpec(
                (1, model, rows), lambda m: (m, 0, 0), pipeline_mode=pl.Buffered(1)
            ),
            inside,
            inside,
            anywhere,
        ],
        out_shape=[
            jax.ShapeDtypeStruct((micro, model, rows), bf16),
            jax.ShapeDtypeStruct((2, shard_rows, hidden), f32),
            jax.ShapeDtypeStruct((shard_rows, hidden), f32),
            jax.ShapeDtypeStruct((dense_rows, width), bf16),
        ],
        scratch_shapes=backward_scratch(heads, inner, model, rows, wide)
        + [
            pltpu.VMEM((slots, 2, kinds, unit_rows, tile), bf16),
            pltpu.VMEM((steps, 2, kinds, unit_rows, tile), bf16),
            pltpu.VMEM((steps, kinds, unit_rows, tile), bf16),
            pltpu.VMEM((steps, row_count - 1, kinds, pad_rows, tile), bf16),
            pltpu.VMEM((2, dense_rows, width), bf16),
            dma((slots, 2)),
            dma((2, steps, 3)),
            dma((2, steps, row_count - 1)),
            dma((landed.shape[0],)),
        ]
        + dense_buffers,
        compiler_params=pltpu.CompilerParams(
            collective_id=2, has_side_effects=True, vmem_limit_bytes=vmem_bytes
        ),
        name="fused_backward",
    )(
        lens, tok, og, residual, back, qkv, attended, log_total, qkv_w, out_w, gains, small,
        bucket, source, landed,
    )


def round_up(value, multiple):
    return -(-value // multiple) * multiple


def shards(
    tokens,
    out_grad,
    lengths,
    offset_bucket,
    qkv_weight,
    out_weight,
    bias_table,
    norm_gains,
    inner_weight,
    outer_weight,
):
    dp_count, row_count, col_count = (lax.axis_size(a) for a in ("dp", "row", "col"))
    shard_count = dp_count * row_count
    micro, rows, model = tokens.shape
    shard_rows = inner_weight.shape[1]
    hidden = inner_weight.shape[2]
    steps = hidden // tile
    heads = bias_table.shape[1]
    bucket_part = bias_table.shape[0]
    bucket_count = bucket_part * dp_count
    inner = out_weight.shape[0]
    part = qkv_weight.shape[0]
    head_rows = 16
    direct = (
        dp_count == 2 and col_count == 4 and part % 32 == 0 and shard_rows % 8 == 0 and steps >= 7
        and micro == 2 and inner % tile == 0 and row_count == 4
    )

    group_rows = shard_rows if direct else model // 2
    pad_rows = round_up(group_rows, 16 if direct else 256)

    tok_t = jnp.transpose(tokens, (0, 2, 1))
    og_t = jnp.transpose(out_grad, (0, 2, 1))
    out_part = out_weight.T
    small_width = round_up(max(part, bucket_part), tile)
    gain_rows = 16
    small = jnp.concatenate(
        [
            jnp.pad(norm_gains, ((0, gain_rows - 2), (0, small_width - part))),
            jnp.pad(bias_table.T, ((0, head_rows - heads), (0, small_width - bucket_part))),
        ],
        axis=0,
    )
    bucket = jnp.pad(offset_bucket[::-1], (0, 1), constant_values=-1)[None, :]
    packed = jnp.stack([inner_weight[0], inner_weight[1], outer_weight.T])
    if direct:
        packed = jnp.pad(packed, ((0, 0), (0, pad_rows - shard_rows), (0, 0)))
        packed = packed.reshape(3, pad_rows, steps, tile).transpose(2, 0, 1, 3)
        (
            normed, normed_t, og_pad, og_pad_t, qkv, attended, log_total, residual, first,
            qkv_full, out_full, small_full, gains,
        ) = fused_forward(
            lengths, tok_t, og_t, bucket, packed, qkv_weight, out_part, small, heads,
            2, group_rows, pad_rows, row_count, col_count, bucket_part,
        )
    else:
        packed = packed.reshape(3, shard_rows, steps, tile).transpose(2, 0, 1, 3)
        weights = lax.all_gather(packed, ("dp", "row"), axis=2, tiled=True)
        weights = jnp.moveaxis(lax.all_gather(weights, "col", axis=0), 0, 1)
        weights = weights.reshape(steps, col_count, 3, 2, group_rows, tile)
        weights = jnp.pad(weights, ((0, 0),) * 4 + ((0, pad_rows - group_rows), (0, 0)))
        weights = weights.reshape(steps, col_count, 3, 2 * pad_rows, tile)
        qkv_full, out_full, small_full = (
            lax.all_gather(a, "dp", axis=0) for a in (qkv_weight, out_part, small)
        )
    qkv_full = qkv_full.reshape(1, model, 3 * inner)
    out_full = out_full.reshape(1, model, inner)
    if direct:
        layer_t, back, sums, _, landed = fused_hidden(
            normed, normed_t, og_pad, og_pad_t, residual, first, packed, micro, model, group_rows,
            pad_rows, row_count, 4,
        )
    else:
        gains = small_full[:, :2, :part].transpose(0, 2, 1).reshape(model, 2).astype(f32)
        table = small_full[:, gain_rows : gain_rows + head_rows, :bucket_part]
        table = table.transpose(1, 0, 2).reshape(head_rows, bucket_count)
        normed, normed_t, og_pad, og_pad_t, qkv, attended, log_total, residual = attention_forward(
            lengths, tok_t, og_t, qkv_full, out_full, gains, table, bucket, heads, group_rows,
            pad_rows,
        )
        layer_t, back, weight_grads = feed_forward(
            normed, normed_t, og_pad, og_pad_t, residual, weights, micro, model, group_rows,
            pad_rows,
        )
    qkv_full, out_full = qkv_full[0], out_full[0]
    backward = (
        lengths, tok_t, og_t, residual, back, qkv, attended, log_total, qkv_full, out_full, gains,
    )
    dense_rows = round_up(part + 32, 64 * row_count)
    if direct:
        tok_grad_t, inner_grad, outer_grad, total = fused_backward(
            *backward, small_full, bucket, sums, landed, dense_rows, group_rows, pad_rows, row_count,
            bucket_part,
        )
    else:
        tok_grad_t, qkv_grad, out_grads, table_grad, gains_grad = attention_backward(
            *backward, table, bucket, group_rows, pad_rows
        )
        width = 4 * inner
        table_part = table_grad.reshape(head_rows, dp_count, bucket_part).transpose(1, 0, 2)
        gains_part = gains_grad.reshape(16, dp_count, part).transpose(1, 0, 2)
        rest = dense_rows - part - 32
        dense = jnp.concatenate([qkv_grad, out_grads], axis=1).reshape(dp_count, part, width)
        dense = jnp.concatenate(
            [
                dense,
                jnp.pad(gains_part, ((0, 0), (0, 0), (0, width - part))),
                jnp.pad(table_part, ((0, 0), (0, rest), (0, width - bucket_part))),
            ],
            axis=1,
        ).astype(bf16)
        grads = weight_grads.reshape(steps, col_count, 3, 2, pad_rows, tile)
        grads = grads[:, :, :, :, :group_rows].reshape(steps, col_count, 3, model, tile)
        grads = jnp.moveaxis(grads, 1, 0)
        grads = lax.psum_scatter(grads, "col", scatter_dimension=0)
        grads = lax.psum_scatter(grads, ("dp", "row"), scatter_dimension=2, tiled=True)
        grads = grads.transpose(1, 2, 0, 3).reshape(3, shard_rows, hidden)
        inner_grad, outer_grad = grads[:2].astype(f32), grads[2].astype(f32)
        total = lax.psum_scatter(dense, "dp", scatter_dimension=0)
        total = lax.psum(total, ("row", "col"))
    total = total.astype(f32)
    return (
        jnp.transpose(layer_t, (0, 2, 1)),
        jnp.transpose(tok_grad_t, (0, 2, 1)),
        total[:part, : 3 * inner],
        total[:part, 3 * inner :].T,
        total[part + 16 : part + 16 + heads, :bucket_part].T,
        total[part : part + 2, :part],
        inner_grad,
        outer_grad.T,
    )


def solution(mesh):
    return jax.shard_map(
        shards,
        mesh=mesh,
        in_specs=(
            P(None, ("dp", "row", "col"), None),
            P(None, ("dp", "row", "col"), None),
            P(None, ("dp", "row", "col"), None),
            P(),
            P("dp", None),
            P(None, "dp"),
            P("dp", None),
            P(None, "dp"),
            P(None, ("dp", "row"), "col"),
            P("col", ("dp", "row")),
        ),
        out_specs=(
            P(None, ("dp", "row", "col"), None),
            P(None, ("dp", "row", "col"), None),
            P("dp", None),
            P(None, "dp"),
            P("dp", None),
            P(None, "dp"),
            P(None, ("dp", "row"), "col"),
            P("col", ("dp", "row")),
        ),
        check_vma=False,
    )
```
